256 devices in a mesh: occ: 8 (over x_hi, y), virt: 32 (over z, x_lo, core).
Axes of the slice: x: 4 (x_hi: 2, x_lo: 2; x = x_hi * 2 + x_lo), y: 4, z: 8, core: 2. Of those that a mesh axis runs over, the one named last changes fastest.
Arguments:
- amplitudes: float32 [24, 24, 384, 384], P('occ', None, 'virt'), may hold values from -6 to 6
- cycle_integrals: bfloat16 [384, 24, 24, 384], P('virt', None, 'occ'), may hold values from -0.0625 to 0.0625
- occ_energy: float32 [24], replicated, may hold values from -2 to -0.5
- virt_energy: float32 [384], replicated, may hold values from 0.2 to 1.5
- occ_irrep: int32 [24], replicated, may hold values from 0 to 3
- virt_irrep: int32 [384], replicated, may hold values from 0 to 3, as said below
Outputs:
- new_amplitudes: float32 [24, 24, 384, 384], P('occ', None, 'virt')
The draws below stay inside these ranges and needn't reach their ends.
Inputs may be any that keep to these rules, and one draw needn't show every extreme that they name: `occ_irrep`: C2v irrep labels; the product of irreps is their exclusive or. `virt_irrep`: C2v irrep labels; the product of irreps is their exclusive or; each of the four irreps labels exactly 96 virtual orbitals.
All inputs are finite; a program needn't handle non-finite values.
Results may differ from the reference program's by a relative error of at most 0.0012.
Values may be sent and summed in bfloat16 or wider, within the bound.
A program may use at most 192 MiB of HBM per device.

```python
import jax
import jax.numpy as jnp
from jax import lax

OCC = 24
VIRT = 384


def draw_virt_irrep(key, part):
    key = jax.random.fold_in(key, 7)
    labels = jnp.repeat(jnp.arange(4, dtype=jnp.int32), VIRT // 4)
    return jax.random.permutation(key, labels)


def with_ends(entries, key, smallest, top_value):
    extent = entries.shape
    place = [jax.random.randint(jax.random.fold_in(key, axis), (), 0, extent[axis]) for axis in range(len(extent))]
    entries = entries.at[tuple(place)].set(smallest)
    longest = extent.index(max(extent))
    place[longest] = (place[longest] + 1) % extent[longest]
    return entries.at[tuple(place)].set(top_value)


def steps_of(rng, shape, shards, smallest, top_value):
    gain, own = 1.0, jax.random.fold_in(rng, 6)
    for dim, blocks in shards:
        draws = jnp.exp(jax.random.uniform(jax.random.fold_in(own, dim), (blocks,), jnp.float32, smallest / len(shards), top_value / len(shards)))
        gain = gain * jnp.repeat(draws, shape[dim] // blocks).reshape([-1 if axis == dim else 1 for axis in range(len(shape))])
    return gain


def noise(stream_key, dims, spread, most, shards=(), held_as=jnp.bfloat16):
    result = spread * jax.random.normal(stream_key, dims, jnp.float32)
    if shards:
        result = result * steps_of(stream_key, dims, shards, -0.22, 0.18)
    return jnp.clip(result, -most, most).astype(held_as)


def setup_inputs(seed: int = 0) -> dict:
    streams_of = jax.random.split(jax.random.key(seed), 7)
    amplitudes = noise(streams_of[0], (OCC, OCC, VIRT, VIRT), 1.0, 6.0, ((0, 8), (2, 32)), jnp.float32)
    cycle_integrals = noise(streams_of[1], (VIRT, OCC, OCC, VIRT), (OCC * VIRT) ** -0.5, 0.0625, ((0, 32), (2, 8)))
    occ_energy = jnp.clip(jax.random.uniform(streams_of[2], (OCC,), jnp.float32, -2.0, -0.5), -2.0, -0.5)
    virt_energy = jnp.clip(jax.random.uniform(streams_of[3], (VIRT,), jnp.float32, 0.2, 1.5), 0.2, 1.5)
    occ_irrep = with_ends(jax.random.randint(streams_of[4], (OCC,), 0, 4), jax.random.fold_in(streams_of[4], 1), 0, 3).astype(jnp.int32)
    virt_irrep = draw_virt_irrep(jax.random.fold_in(streams_of[6], 71), 0)
    return {"amplitudes": amplitudes, "cycle_integrals": cycle_integrals, "occ_energy": occ_energy, "virt_energy": virt_energy, "occ_irrep": occ_irrep, "virt_irrep": virt_irrep}


def irrep_mask(occ_rows, occ_labels, virt_rows, virt_labels):
    combined = jnp.bitwise_xor(jnp.bitwise_xor(occ_rows[:, None, None, None], occ_labels[None, :, None, None]), jnp.bitwise_xor(virt_rows[None, None, :, None], virt_labels[None, None, None, :]))
    return (combined == 0).astype(jnp.float32)


def reference(amplitudes, cycle_integrals, occ_energy, virt_energy, occ_irrep, virt_irrep):
    allowed = irrep_mask(occ_irrep, occ_irrep, virt_irrep, virt_irrep)
    amps_low = (amplitudes * allowed).astype(jnp.bfloat16)
    wmatrix = jnp.transpose(cycle_integrals, (2, 3, 1, 0)).reshape(OCC * VIRT, OCC * VIRT)

    def one_row(row_amps):
        left = jnp.transpose(row_amps, (1, 0, 2)).reshape(VIRT, OCC * VIRT)
        product = jnp.dot(left, wmatrix, preferred_element_type=jnp.float32)
        return jnp.transpose(product.reshape(VIRT, OCC, VIRT), (1, 0, 2))

    cycle = lax.map(one_row, amps_low)
    resid = cycle - jnp.transpose(cycle, (1, 0, 2, 3))
    denom = occ_energy[:, None, None, None] + occ_energy[None, :, None, None] - virt_energy[None, None, :, None] - virt_energy[None, None, None, :]
    return allowed * (amplitudes + resid / denom)
```

```python
import jax
import jax.numpy as jnp
from jax import lax
from jax.experimental import pallas as pl
from jax.experimental.pallas import tpu as pltpu
from jax.sharding import PartitionSpec as P

F32, BF16, I32 = jnp.float32, jnp.bfloat16, jnp.int32
MESH = pl.DeviceIdType.MESH
VMEM_LIMIT = 48 * 1024 * 1024


def iota(shape, dim):
    return lax.broadcasted_iota(I32, shape, dim)


def quot(x, d):
    s = 20
    return (x * (-(-(1 << s) // d))) >> s


def parts_of(x, d):
    q = quot(x, d)
    return q, x - q * d


def one_hot(mask):
    return jnp.where(mask, 1.0, 0.0).astype(BF16)


def pick(row, index):
    lanes = iota((index.shape[0], row.shape[1]), 1)
    return jnp.sum(jnp.where(lanes == index, row, 0.0), axis=1, keepdims=True)


def dot_nn(a, b):
    return lax.dot_general(a, b, (((1,), (0,)), ((), ())), preferred_element_type=F32)


def dot_nt(a, b):
    return lax.dot_general(a, b, (((1,), (1,)), ((), ())), preferred_element_type=F32)


def pack_kernel(amps, ints, occ_s, occ_r, virt_r, tsend, wsend, rank_out, rows):
    o, v = lax.axis_index("occ"), lax.axis_index("virt")
    y = lax.rem(o, 4)
    virt = virt_r[...]
    virtf = virt.astype(F32)
    occf = occ_r[...].astype(F32)
    r0, c0 = iota((384, 384), 0), iota((384, 384), 1)
    vcol = jnp.sum(jnp.where(r0 == c0, virtf, 0.0), axis=1, keepdims=True)
    rank = jnp.sum(jnp.where((vcol == virtf) & (r0 < c0), 1.0, 0.0), axis=0, keepdims=True)
    rank_out[...] = jnp.broadcast_to(rank, (8, 384))
    ranki = rank.astype(I32)

    b, j = parts_of(iota((288, 1), 0), 24)
    label = pick(virtf, v * 12 + b).astype(I32) ^ pick(occf, j).astype(I32)
    total = jnp.zeros((288, 384), F32)
    for k in range(3):
        w = ints[:, k].astype(F32).reshape(288, 384)
        w = jnp.where((label ^ occ_s[3 * o + k]) == virt, w, 0.0).astype(BF16)
        total += dot_nt(w, one_hot(r0 == ranki + (96 * k + 32 * y)))
    od, r = parts_of(iota((384, 1), 0), 48)
    jl, bb = r >> 4, r & 15
    source = jnp.where(bb < 12, bb * 24 + 3 * od + jl, -1)
    wsend[...] = dot_nn(one_hot(iota((384, 288), 1) == source), total.astype(BF16)).astype(BF16).reshape(8, 48, 384)

    ia, q = parts_of(iota((216, 1), 0), 6)
    i, a = parts_of(ia, 12)
    label = pick(virtf, v * 12 + a).astype(I32) ^ pick(occf, 3 * o + i).astype(I32)
    for lane in range(3):
        rows[lane] = amps[:, lane * 128 : lane * 128 + 128]
    total = jnp.zeros((216, 384), F32)
    for kk in range(4):
        t = jnp.concatenate([rows[lane, pl.ds(kk, 216, stride=4), :] for lane in range(3)], axis=1)
        t = jnp.where((label ^ pick(occf, 4 * q + kk).astype(I32)) == virt, t, 0.0).astype(BF16)
        total += dot_nt(t, one_hot(r0 == ranki + 96 * kk))
    qd, r = parts_of(iota((288, 1), 0), 48)
    il, aa = r >> 4, r & 15
    source = jnp.where(aa < 12, (il * 12 + aa) * 6 + qd, -1)
    t = dot_nn(one_hot(iota((288, 216), 1) == source), total.astype(BF16)).astype(BF16)
    for q in range(6):
        tsend[q // 3, :, (q % 3) * 384 : (q % 3 + 1) * 384] = t[q * 48 : (q + 1) * 48]


def cycle_kernel(
    tsend, wsend, occ_s, occ_r, virt_r, rank_r, resid,
    wstage, tbuf, wring, place, labels, rpart, rpeer, full, dsend, dbuf,
    w_send, w_recv, t_send, t_recv, ring_send, ring_recv, sib_send, sib_recv,
    r_send, r_recv, d_send, d_recv,
):
    o, v = lax.axis_index("occ"), lax.axis_index("virt")
    xh, y = o // 4, lax.rem(o, 4)
    z, s = v // 4, lax.rem(v, 4)
    xl, core = s // 2, lax.rem(s, 2)
    step = 1 - 2 * core
    znext = lax.rem(z + step + 8, 8)
    zback = lax.rem(z - step + 8, 8)

    barrier = pltpu.get_barrier_semaphore()
    for sd in range(4):
        def greet(d, _, sd=sd):
            pl.semaphore_signal(barrier, inc=1, device_id=(lax.rem(o + d, 8), z * 4 + lax.rem(s + sd, 4)), device_id_type=MESH)
            return 0
        lax.fori_loop(1 if sd == 0 else 0, 8, greet, 0)
    for zd in (znext, zback):
        pl.semaphore_signal(barrier, inc=1, device_id=(o, zd * 4 + s), device_id_type=MESH)
    pl.semaphore_wait(barrier, 33)

    def w_copy(d, c):
        od = lax.rem(o + d, 8)
        return pltpu.make_async_remote_copy(
            src_ref=wsend.at[od], dst_ref=wstage.at[y * 4 + s], send_sem=w_send, recv_sem=w_recv,
            device_id=(od, z * 4 + xh * 2 + c), device_id_type=MESH,
        )

    w_local = pltpu.make_async_copy(wsend.at[o], wstage.at[y * 4 + s], w_recv)
    for c in range(2):
        own = (xh == xl) & (core == c)

        @pl.when(own)
        def _():
            w_local.start()

        @pl.when(jnp.logical_not(own))
        def _(c=c):
            w_copy(0, c).start()

    def w_start(d, _):
        w_copy(d, 0).start()
        w_copy(d, 1).start()
        return 0

    lax.fori_loop(1, 8, w_start, 0)

    def t_copy(d, x):
        xd = lax.rem(xl + x, 2)
        return pltpu.make_async_remote_copy(
            src_ref=tsend.at[xd], dst_ref=tbuf.at[o, xl], send_sem=t_send, recv_sem=t_recv,
            device_id=(lax.rem(o + d, 8), z * 4 + xd * 2 + core), device_id_type=MESH,
        )

    t_local = pltpu.make_async_copy(tsend.at[xl], tbuf.at[o, xl], t_recv)
    t_local.start()
    t_copy(0, 1).start()

    def t_start(d, _):
        t_copy(d, 0).start()
        t_copy(d, 1).start()
        return 0

    lax.fori_loop(1, 8, t_start, 0)

    n = iota((1, 1152), 1)
    zz, r = parts_of(n, 144)
    jl, b48 = parts_of(r, 48)
    values = jnp.concatenate([rank_r[0:4, :], jnp.broadcast_to(virt_r[...].astype(F32), (4, 384))], axis=0)
    spread = dot_nn(values.astype(BF16), one_hot(iota((384, 1152), 0) == zz * 48 + b48)).astype(I32)
    place[...] = one_hot(iota((384, 1152), 0) == spread[0:1, :] + jl * 128)
    oj = jnp.where(jl == 0, occ_s[3 * o], jnp.where(jl == 1, occ_s[3 * o + 1], occ_s[3 * o + 2]))
    labels[...] = jnp.broadcast_to(spread[4:5, :] ^ oj, (8, 1152))

    row = iota((144, 1), 0)
    jr, br = parts_of(row, 48)
    sr, bl = parts_of(br, 12)
    gather = one_hot(iota((144, 192), 1) == sr * 48 + jr * 16 + bl)
    pltpu.make_async_copy(wstage, wstage, w_recv).wait()
    last = None
    for yy in range(4):
        piece = dot_nn(gather, wstage[yy * 4 : yy * 4 + 4].reshape(192, 384))
        first = piece[:, 0:128] if last is None else piece[:, 0:128] + last
        wring[z, :, yy * 256 : yy * 256 + 128] = first.astype(BF16)
        wring[z, :, yy * 256 + 128 : yy * 256 + 256] = piece[:, 128:256].astype(BF16)
        last = piece[:, 256:384]
    wring[z, :, 1024:1152] = last.astype(BF16)

    def ring_copy(t, rows):
        block = lax.rem(z - step * (t - 1) + 8, 8)
        return pltpu.make_async_remote_copy(
            src_ref=wring.at[block, rows], dst_ref=wring.at[block, rows],
            send_sem=ring_send.at[t - 1], recv_sem=ring_recv.at[t - 1],
            device_id=(o, znext * 4 + s), device_id_type=MESH,
        )

    def arrival(t, rows):
        block = lax.rem(z - step * t + 8, 8)
        return pltpu.make_async_copy(wring.at[block, rows], wring.at[block, rows], ring_recv.at[t - 1])

    def sib_copy(t, rows):
        block = lax.rem(z - step * t + 8, 8)
        return pltpu.make_async_remote_copy(
            src_ref=wring.at[block, rows], dst_ref=wring.at[block, rows],
            send_sem=sib_send.at[t - 1], recv_sem=sib_recv.at[t - 1],
            device_id=(o, z * 4 + xl * 2 + 1 - core), device_id_type=MESH,
        )

    def sib_arrival(t, rows):
        block = lax.rem(z + step * t + 8, 8)
        return pltpu.make_async_copy(wring.at[block, rows], wring.at[block, rows], sib_recv.at[t - 1])

    whole, lower, upper = pl.ds(0, 144), pl.ds(0, 80), pl.ds(80, 64)
    ring_copy(1, whole).start()
    for t in (1, 2):
        arrival(t, whole).wait()
        ring_copy(t + 1, whole).start()
        sib_copy(t, whole).start()
    arrival(3, whole).wait()
    for c, rows in ((0, lower), (1, upper)):
        @pl.when(core == c)
        def _(rows=rows):
            ring_copy(4, rows).start()
    sib_copy(3, whole).start()
    for c, rows, others in ((0, lower, upper), (1, upper, lower)):
        @pl.when(core == c)
        def _(rows=rows, others=others):
            arrival(4, rows).wait()
            sib_copy(4, rows).start()
            sib_arrival(4, others).wait()
    for t in (1, 2, 3):
        sib_arrival(t, whole).wait()

    pltpu.make_async_copy(tbuf, tbuf, t_recv).wait()

    virtf = virt_r[...].astype(F32)
    occf = occ_r[...].astype(F32)

    def r_copy(c):
        p = lax.rem(o // 2 + c, 4)
        return pltpu.make_async_remote_copy(
            src_ref=rpart.at[1 - xl, pl.ds(2 * p, 2)], dst_ref=rpeer.at[pl.ds(2 * p, 2)],
            send_sem=r_send.at[c], recv_sem=r_recv.at[c],
            device_id=(o, z * 4 + (1 - xl) * 2 + core), device_id_type=MESH,
        )

    def product(c, _):
        p = lax.rem(o // 2 + c, 4)
        left = tbuf[pl.ds(2 * p, 2)].reshape(192, 1152)
        block, r = parts_of(iota((192, 1), 0), 48)
        a = z * 48 + (block & 1) * 24 + core * 12 + (r & 15)
        i = 6 * p + 3 * (block >> 1) + (r >> 4)
        label = pick(virtf, a).astype(I32) ^ pick(occf, i).astype(I32)
        raw = dot_nt(left, wring[...].reshape(1152, 1152))
        raw = jnp.where(label == labels[0:1, :], raw, 0.0).astype(BF16)
        packed = dot_nt(raw, place[...]).astype(BF16)
        for u in range(2):
            for x in range(2):
                at = (u * 2 + x) * 48
                rpart[x, 2 * p + u] = packed[at : at + 48]
        r_copy(c).start()
        return 0

    lax.fori_loop(0, 4, product, 0)

    def d_copy(od):
        return pltpu.make_async_remote_copy(
            src_ref=dsend.at[od], dst_ref=dbuf.at[o], send_sem=d_send, recv_sem=d_recv,
            device_id=(od, v), device_id_type=MESH,
        )

    d_local = pltpu.make_async_copy(dsend.at[o], dbuf.at[o], d_recv)

    def combine(c, _):
        p = lax.rem(o // 2 + c, 4)
        r_copy(c).wait_recv()
        both = rpart[xl, pl.ds(2 * p, 2)].astype(F32) + rpeer[pl.ds(2 * p, 2)].astype(F32)
        full[pl.ds(2 * p, 2)] = both
        dsend[pl.ds(2 * p, 2)] = both.astype(BF16)
        for u in range(2):
            od = 2 * p + u

            @pl.when(od == o)
            def _():
                d_local.start()

            @pl.when(od != o)
            def _(od=od):
                d_copy(od).start()
        return 0

    lax.fori_loop(0, 4, combine, 0)
    pltpu.make_async_copy(dbuf, dbuf, d_recv).wait()

    def subtract(g, _):
        for i in range(3):
            for j in range(3):
                direct = dbuf[g, i * 16 : i * 16 + 16, j * 128 : j * 128 + 128].astype(F32)
                mirror = full[g, j * 16 : j * 16 + 16, i * 128 : i * 128 + 128]
                resid[g, i * 16 : i * 16 + 16, j * 128 : j * 128 + 128] = direct - mirror
        return 0

    lax.fori_loop(0, 8, subtract, 0)

    for c in range(2):
        @pl.when(jnp.logical_not((xh == xl) & (core == c)))
        def _(c=c):
            w_copy(0, c).wait_send()

    def sent(d, _):
        w_copy(d, 0).wait_send()
        w_copy(d, 1).wait_send()
        t_copy(d, 0).wait_send()
        t_copy(d, 1).wait_send()
        d_copy(lax.rem(o + d, 8)).wait_send()
        return 0

    lax.fori_loop(1, 8, sent, 0)
    t_copy(0, 1).wait_send()
    for t in (1, 2, 3):
        ring_copy(t, whole).wait_send()
        sib_copy(t, whole).wait_send()
    for c, rows in ((0, lower), (1, upper)):
        @pl.when(core == c)
        def _(rows=rows):
            ring_copy(4, rows).wait_send()
            sib_copy(4, rows).wait_send()
    for c in range(4):
        r_copy(c).wait_send()


def update_kernel(amps, resid, occ_r, virt_r, rank_r, occ_e, virt_e, out, spread):
    o, v = lax.axis_index("occ"), lax.axis_index("virt")
    virt = virt_r[...]
    occf, virtf = occ_r[...].astype(F32), virt.astype(F32)
    expand = one_hot(iota((128, 384), 0) == rank_r[0:1, :].astype(I32))
    for g in range(8):
        for jl in range(3):
            x = resid[g, :, jl * 128 : jl * 128 + 128]
            high = x.astype(BF16)
            low = (x - high.astype(F32)).astype(BF16)
            e = dot_nn(high, expand) + dot_nn(low, expand)
            for i in range(3):
                for lane in range(3):
                    spread[lane, pl.ds(i * 288 + 3 * g + jl, 12, stride=24), :] = e[i * 16 : i * 16 + 12, lane * 128 : lane * 128 + 128]
    for i in range(3):
        a, j = parts_of(iota((288, 1), 0), 24)
        at = pl.ds(i * 288, 288)
        label = pick(virtf, v * 12 + a).astype(I32) ^ pick(occf, j).astype(I32) ^ pick(occf, jnp.full((288, 1), 3 * o + i)).astype(I32)
        energy = pick(occ_e[...], jnp.full((288, 1), 3 * o + i)) + pick(occ_e[...], j) - pick(virt_e[...], v * 12 + a)
        denom = energy - virt_e[...]
        change = jnp.concatenate([spread[lane, at, :] for lane in range(3)], axis=1)
        out[at, :] = jnp.where(label == virt, amps[at, :] + change / denom, 0.0)


def local(amplitudes, cycle_integrals, occ_energy, virt_energy, occ_irrep, virt_irrep):
    vmem = pl.BlockSpec(memory_space=pltpu.VMEM)
    smem = pl.BlockSpec(memory_space=pltpu.SMEM)
    amps = jnp.transpose(amplitudes, (0, 2, 1, 3)).reshape(864, 384)
    ints = jnp.transpose(cycle_integrals, (0, 2, 1, 3))
    occ_r, virt_r = occ_irrep.reshape(1, 24), virt_irrep.reshape(1, 384)
    params = pltpu.CompilerParams(vmem_limit_bytes=VMEM_LIMIT)
    tsend, wsend, rank = pl.pallas_call(
        pack_kernel,
        out_shape=(
            jax.ShapeDtypeStruct((2, 48, 1152), BF16),
            jax.ShapeDtypeStruct((8, 48, 384), BF16),
            jax.ShapeDtypeStruct((8, 384), F32),
        ),
        in_specs=[vmem, vmem, smem, vmem, vmem],
        out_specs=(vmem, vmem, vmem),
        scratch_shapes=[pltpu.VMEM((3, 864, 128), F32)],
        compiler_params=params,
    )(amps, ints, occ_irrep, occ_r, virt_r)
    dma = pltpu.SemaphoreType.DMA
    resid = pl.pallas_call(
        cycle_kernel,
        out_shape=jax.ShapeDtypeStruct((8, 48, 384), F32),
        in_specs=[vmem, vmem, smem, vmem, vmem, vmem],
        out_specs=vmem,
        scratch_shapes=[
            pltpu.VMEM((16, 48, 384), BF16),
            pltpu.VMEM((8, 2, 48, 1152), BF16),
            pltpu.VMEM((8, 144, 1152), BF16),
            pltpu.VMEM((384, 1152), BF16),
            pltpu.VMEM((8, 1152), I32),
            pltpu.VMEM((2, 8, 48, 384), BF16),
            pltpu.VMEM((8, 48, 384), BF16),
            pltpu.VMEM((8, 48, 384), F32),
            pltpu.VMEM((8, 48, 384), BF16),
            pltpu.VMEM((8, 48, 384), BF16),
            dma, dma, dma, dma, dma((4,)), dma((4,)), dma((4,)), dma((4,)),
            dma((4,)), dma((4,)), dma, dma,
        ],
        compiler_params=pltpu.CompilerParams(
            collective_id=0, has_side_effects=True, vmem_limit_bytes=VMEM_LIMIT
        ),
    )(tsend, wsend, occ_irrep, occ_r, virt_r, rank)
    out = pl.pallas_call(
        update_kernel,
        out_shape=jax.ShapeDtypeStruct((864, 384), F32),
        in_specs=[vmem] * 7,
        out_specs=vmem,
        scratch_shapes=[pltpu.VMEM((3, 864, 128), F32)],
        compiler_params=params,
    )(amps, resid, occ_r, virt_r, rank, occ_energy.reshape(1, 24), virt_energy.reshape(1, 384))
    return jnp.transpose(out.reshape(3, 12, 24, 384), (0, 2, 1, 3))


def solution(mesh):
    return jax.shard_map(
        local,
        mesh=mesh,
        in_specs=(P("occ", None, "virt", None), P("virt", None, "occ", None), P(), P(), P(), P()),
        out_specs=P("occ", None, "virt", None),
        check_vma=False,
    )
```

```python
import jax
import jax.numpy as jnp
from jax import lax
from jax.experimental import pallas as pl
from jax.experimental.pallas import tpu as pltpu
from jax.sharding import PartitionSpec as P

F32, BF16, I32 = jnp.float32, jnp.bfloat16, jnp.int32
MESH = pl.DeviceIdType.MESH
VMEM_LIMIT = 48 * 1024 * 1024


def iota(shape, dim):
    return lax.broadcasted_iota(I32, shape, dim)


def quot(x, d):
    s = 20
    return (x * (-(-(1 << s) // d))) >> s


def parts_of(x, d):
    q = quot(x, d)
    return q, x - q * d


def one_hot(mask):
    return jnp.where(mask, 1.0, 0.0).astype(BF16)


def pick(row, index):
    lanes = iota((index.shape[0], row.shape[1]), 1)
    return jnp.sum(jnp.where(lanes == index, row, 0.0), axis=1, keepdims=True)


def dot_nn(a, b):
    return lax.dot_general(a, b, (((1,), (0,)), ((), ())), preferred_element_type=F32)


def dot_nt(a, b):
    return lax.dot_general(a, b, (((1,), (1,)), ((), ())), preferred_element_type=F32)


def pack_kernel(amps, ints, occ_s, occ_r, virt_r, tsend, wsend, rank_out, rows):
    o, v = lax.axis_index("occ"), lax.axis_index("virt")
    y = lax.rem(o, 4)
    virt = virt_r[...]
    virtf = virt.astype(F32)
    occf = occ_r[...].astype(F32)
    r0, c0 = iota((384, 384), 0), iota((384, 384), 1)
    vcol = jnp.sum(jnp.where(r0 == c0, virtf, 0.0), axis=1, keepdims=True)
    rank = jnp.sum(jnp.where((vcol == virtf) & (r0 < c0), 1.0, 0.0), axis=0, keepdims=True)
    rank_out[...] = jnp.broadcast_to(rank, (8, 384))
    ranki = rank.astype(I32)

    b, j = parts_of(iota((288, 1), 0), 24)
    label = pick(virtf, v * 12 + b).astype(I32) ^ pick(occf, j).astype(I32)
    total = jnp.zeros((288, 384), F32)
    for k in range(3):
        w = ints[:, k].astype(F32).reshape(288, 384)
        w = jnp.where((label ^ occ_s[3 * o + k]) == virt, w, 0.0).astype(BF16)
        total += dot_nt(w, one_hot(r0 == ranki + (96 * k + 32 * y)))
    od, r = parts_of(iota((384, 1), 0), 48)
    jl, bb = r >> 4, r & 15
    source = jnp.where(bb < 12, bb * 24 + 3 * od + jl, -1)
    wsend[...] = dot_nn(one_hot(iota((384, 288), 1) == source), total.astype(BF16)).astype(BF16).reshape(8, 48, 384)

    ia, q = parts_of(iota((216, 1), 0), 6)
    i, a = parts_of(ia, 12)
    label = pick(virtf, v * 12 + a).astype(I32) ^ pick(occf, 3 * o + i).astype(I32)
    for lane in range(3):
        rows[lane] = amps[:, lane * 128 : lane * 128 + 128]
    total = jnp.zeros((216, 384), F32)
    for kk in range(4):
        t = jnp.concatenate([rows[lane, pl.ds(kk, 216, stride=4), :] for lane in range(3)], axis=1)
        t = jnp.where((label ^ pick(occf, 4 * q + kk).astype(I32)) == virt, t, 0.0).astype(BF16)
        total += dot_nt(t, one_hot(r0 == ranki + 96 * kk))
    qd, r = parts_of(iota((288, 1), 0), 48)
    il, aa = r >> 4, r & 15
    source = jnp.where(aa < 12, (il * 12 + aa) * 6 + qd, -1)
    t = dot_nn(one_hot(iota((288, 216), 1) == source), total.astype(BF16)).astype(BF16)
    for q in range(6):
        tsend[q // 3, :, (q % 3) * 384 : (q % 3 + 1) * 384] = t[q * 48 : (q + 1) * 48]


def cycle_kernel(
    tsend, wsend, occ_s, occ_r, virt_r, rank_r, resid,
    wstage, tbuf, wring, place, labels, rpart, rpeer, full, dsend, dbuf,
    w_send, w_recv, ws_send, ws_recv, t_send, t_recv, ring_send, ring_recv, sib_send, sib_recv,
    r_send, r_recv, d_send, d_recv,
):
    o, v = lax.axis_index("occ"), lax.axis_index("virt")
    xh, y = o // 4, lax.rem(o, 4)
    z, s = v // 4, lax.rem(v, 4)
    xl, core = s // 2, lax.rem(s, 2)
    step = 1 - 2 * core
    znext = lax.rem(z + step + 8, 8)
    zback = lax.rem(z - step + 8, 8)

    barrier = pltpu.get_barrier_semaphore()
    for sd in range(4):
        def greet(d, _, sd=sd):
            pl.semaphore_signal(barrier, inc=1, device_id=(lax.rem(o + d, 8), z * 4 + lax.rem(s + sd, 4)), device_id_type=MESH)
            return 0
        lax.fori_loop(1 if sd == 0 else 0, 8, greet, 0)
    for zd in (znext, zback):
        pl.semaphore_signal(barrier, inc=1, device_id=(o, zd * 4 + s), device_id_type=MESH)
    pl.semaphore_wait(barrier, 33)

    def w_copy(d):
        od = lax.rem(o + d, 8)
        return pltpu.make_async_remote_copy(
            src_ref=wsend.at[od], dst_ref=wstage.at[core, y * 2 + xl], send_sem=w_send, recv_sem=w_recv,
            device_id=(od, z * 4 + xh * 2 + core), device_id_type=MESH,
        )

    @pl.when(xh == xl)
    def _():
        pltpu.make_async_copy(wsend.at[o], wstage.at[core, y * 2 + xl], w_recv).start()

    @pl.when(xh != xl)
    def _():
        w_copy(0).start()

    def w_start(d, _):
        w_copy(d).start()
        return 0

    lax.fori_loop(1, 8, w_start, 0)

    def t_copy(d, x):
        xd = lax.rem(xl + x, 2)
        return pltpu.make_async_remote_copy(
            src_ref=tsend.at[xd], dst_ref=tbuf.at[o, xl], send_sem=t_send, recv_sem=t_recv,
            device_id=(lax.rem(o + d, 8), z * 4 + xd * 2 + core), device_id_type=MESH,
        )

    t_local = pltpu.make_async_copy(tsend.at[xl], tbuf.at[o, xl], t_recv)
    t_local.start()
    t_copy(0, 1).start()

    def t_start(d, _):
        t_copy(d, 0).start()
        t_copy(d, 1).start()
        return 0

    lax.fori_loop(1, 8, t_start, 0)

    n = iota((1, 1152), 1)
    zz, r = parts_of(n, 144)
    jl, b48 = parts_of(r, 48)
    values = jnp.concatenate([rank_r[0:4, :], jnp.broadcast_to(virt_r[...].astype(F32), (4, 384))], axis=0)
    spread = dot_nn(values.astype(BF16), one_hot(iota((384, 1152), 0) == zz * 48 + b48)).astype(I32)
    place[...] = one_hot(iota((384, 1152), 0) == spread[0:1, :] + jl * 128)
    oj = jnp.where(jl == 0, occ_s[3 * o], jnp.where(jl == 1, occ_s[3 * o + 1], occ_s[3 * o + 2]))
    labels[...] = jnp.broadcast_to(spread[4:5, :] ^ oj, (8, 1152))

    row = iota((144, 1), 0)
    jr, br = parts_of(row, 48)
    sr, bl = parts_of(br, 12)
    gather = one_hot(iota((144, 192), 1) == (sr & 1) * 96 + (sr >> 1) * 48 + jr * 16 + bl)
    w_share = pltpu.make_async_remote_copy(
        src_ref=wstage.at[core], dst_ref=wstage.at[core], send_sem=ws_send, recv_sem=ws_recv,
        device_id=(o, z * 4 + xl * 2 + 1 - core), device_id_type=MESH,
    )
    pltpu.make_async_copy(wstage.at[core], wstage.at[core], w_recv).wait()
    w_share.start()
    pltpu.make_async_copy(wstage.at[1 - core], wstage.at[1 - core], ws_recv).wait()
    last = None
    for yy in range(4):
        piece = dot_nn(gather, wstage[:, yy * 2 : yy * 2 + 2].reshape(192, 384))
        first = piece[:, 0:128] if last is None else piece[:, 0:128] + last
        wring[z, :, yy * 256 : yy * 256 + 128] = first.astype(BF16)
        wring[z, :, yy * 256 + 128 : yy * 256 + 256] = piece[:, 128:256].astype(BF16)
        last = piece[:, 256:384]
    wring[z, :, 1024:1152] = last.astype(BF16)

    def piece_of(block, start, size):
        return wring.at[lax.rem(block + 8, 8), pl.ds(pl.multiple_of(start, 16), size)]

    def first_row(g, c):
        return 48 * g + c * (96 - 96 * g)

    def ring_copy(t, g, start, size=48):
        ref = piece_of(z - step * (t - 1), start, size)
        n = 3 * t - 3 + g
        return pltpu.make_async_remote_copy(
            src_ref=ref, dst_ref=ref, send_sem=ring_send.at[n], recv_sem=ring_recv.at[n],
            device_id=(o, znext * 4 + s), device_id_type=MESH,
        )

    def sib_copy(t, g, start, size=48):
        ref = piece_of(z - step * t, start, size)
        n = 3 * t - 3 + g
        return pltpu.make_async_remote_copy(
            src_ref=ref, dst_ref=ref, send_sem=sib_send.at[n], recv_sem=sib_recv.at[n],
            device_id=(o, z * 4 + xl * 2 + 1 - core), device_id_type=MESH,
        )

    def arrived(t, g, sems, way, start, size=48):
        ref = piece_of(z - way * t, start, size)
        pltpu.make_async_copy(ref, ref, sems.at[3 * t - 3 + g]).wait()

    rest = ((48, 32), (80, 16))
    for g in range(3):
        ring_copy(1, g, first_row(g, core)).start()
    for t in range(1, 4):
        for g in range(3):
            start = first_row(g, core)
            arrived(t, g, ring_recv, step, start)
            if t < 3 or g == 0:
                ring_copy(t + 1, g, start).start()
            elif g == 1:
                for c in range(2):
                    @pl.when(core == c)
                    def _(c=c):
                        ring_copy(4, 1, *rest[c]).start()
            sib_copy(t, g, start).start()
    arrived(4, 0, ring_recv, step, first_row(0, core))
    sib_copy(4, 0, first_row(0, core)).start()
    for c in range(2):
        @pl.when(core == c)
        def _(c=c):
            arrived(4, 1, ring_recv, step, *rest[c])
            sib_copy(4, 1, *rest[c]).start()
            arrived(4, 1, sib_recv, -step, *rest[1 - c])
    for t in range(1, 5):
        for g in range(3 if t < 4 else 1):
            arrived(t, g, sib_recv, -step, first_row(g, 1 - core))

    pltpu.make_async_copy(tbuf, tbuf, t_recv).wait()

    virtf = virt_r[...].astype(F32)
    occf = occ_r[...].astype(F32)

    def r_copy(c):
        p = lax.rem(o // 2 + c, 4)
        return pltpu.make_async_remote_copy(
            src_ref=rpart.at[1 - xl, pl.ds(2 * p, 2)], dst_ref=rpeer.at[pl.ds(2 * p, 2)],
            send_sem=r_send.at[c], recv_sem=r_recv.at[c],
            device_id=(o, z * 4 + (1 - xl) * 2 + core), device_id_type=MESH,
        )

    def product(c, _):
        p = lax.rem(o // 2 + c, 4)
        left = tbuf[pl.ds(2 * p, 2)].reshape(192, 1152)
        block, r = parts_of(iota((192, 1), 0), 48)
        a = z * 48 + (block & 1) * 24 + core * 12 + (r & 15)
        i = 6 * p + 3 * (block >> 1) + (r >> 4)
        label = pick(virtf, a).astype(I32) ^ pick(occf, i).astype(I32)
        raw = dot_nt(left, wring[...].reshape(1152, 1152))
        raw = jnp.where(label == labels[0:1, :], raw, 0.0).astype(BF16)
        packed = dot_nt(raw, place[...]).astype(BF16)
        for u in range(2):
            for x in range(2):
                at = (u * 2 + x) * 48
                rpart[x, 2 * p + u] = packed[at : at + 48]
        r_copy(c).start()
        return 0

    lax.fori_loop(0, 4, product, 0)

    def d_copy(od):
        return pltpu.make_async_remote_copy(
            src_ref=dsend.at[od], dst_ref=dbuf.at[o], send_sem=d_send, recv_sem=d_recv,
            device_id=(od, v), device_id_type=MESH,
        )

    d_local = pltpu.make_async_copy(dsend.at[o], dbuf.at[o], d_recv)

    def combine(c, _):
        p = lax.rem(o // 2 + c, 4)
        r_copy(c).wait_recv()
        both = rpart[xl, pl.ds(2 * p, 2)].astype(F32) + rpeer[pl.ds(2 * p, 2)].astype(F32)
        full[pl.ds(2 * p, 2)] = both
        dsend[pl.ds(2 * p, 2)] = both.astype(BF16)
        for u in range(2):
            od = 2 * p + u

            @pl.when(od == o)
            def _():
                d_local.start()

            @pl.when(od != o)
            def _(od=od):
                d_copy(od).start()
        return 0

    lax.fori_loop(0, 4, combine, 0)
    pltpu.make_async_copy(dbuf, dbuf, d_recv).wait()

    def subtract(g, _):
        for i in range(3):
            for j in range(3):
                direct = dbuf[g, i * 16 : i * 16 + 16, j * 128 : j * 128 + 128].astype(F32)
                mirror = full[g, j * 16 : j * 16 + 16, i * 128 : i * 128 + 128]
                resid[g, i * 16 : i * 16 + 16, j * 128 : j * 128 + 128] = direct - mirror
        return 0

    lax.fori_loop(0, 8, subtract, 0)

    @pl.when(xh != xl)
    def _():
        w_copy(0).wait_send()

    def sent(d, _):
        w_copy(d).wait_send()
        t_copy(d, 0).wait_send()
        t_copy(d, 1).wait_send()
        d_copy(lax.rem(o + d, 8)).wait_send()
        return 0

    lax.fori_loop(1, 8, sent, 0)
    t_copy(0, 1).wait_send()
    w_share.wait_send()
    for t in range(1, 5):
        for g in range(3 if t < 4 else 1):
            ring_copy(t, g, first_row(g, core)).wait_send()
            sib_copy(t, g, first_row(g, core)).wait_send()
    for c in range(2):
        @pl.when(core == c)
        def _(c=c):
            ring_copy(4, 1, *rest[c]).wait_send()
            sib_copy(4, 1, *rest[c]).wait_send()
    for c in range(4):
        r_copy(c).wait_send()


def update_kernel(amps, resid, occ_r, virt_r, rank_r, occ_e, virt_e, out, spread):
    o, v = lax.axis_index("occ"), lax.axis_index("virt")
    virt = virt_r[...]
    occf, virtf = occ_r[...].astype(F32), virt.astype(F32)
    expand = one_hot(iota((128, 384), 0) == rank_r[0:1, :].astype(I32))
    for g in range(8):
        for jl in range(3):
            x = resid[g, :, jl * 128 : jl * 128 + 128]
            high = x.astype(BF16)
            low = (x - high.astype(F32)).astype(BF16)
            e = dot_nn(high, expand) + dot_nn(low, expand)
            for i in range(3):
                for lane in range(3):
                    spread[lane, pl.ds(i * 288 + 3 * g + jl, 12, stride=24), :] = e[i * 16 : i * 16 + 12, lane * 128 : lane * 128 + 128]
    for i in range(3):
        a, j = parts_of(iota((288, 1), 0), 24)
        at = pl.ds(i * 288, 288)
        label = pick(virtf, v * 12 + a).astype(I32) ^ pick(occf, j).astype(I32) ^ pick(occf, jnp.full((288, 1), 3 * o + i)).astype(I32)
        energy = pick(occ_e[...], jnp.full((288, 1), 3 * o + i)) + pick(occ_e[...], j) - pick(virt_e[...], v * 12 + a)
        denom = energy - virt_e[...]
        change = jnp.concatenate([spread[lane, at, :] for lane in range(3)], axis=1)
        out[at, :] = jnp.where(label == virt, amps[at, :] + change / denom, 0.0)


def local(amplitudes, cycle_integrals, occ_energy, virt_energy, occ_irrep, virt_irrep):
    vmem = pl.BlockSpec(memory_space=pltpu.VMEM)
    smem = pl.BlockSpec(memory_space=pltpu.SMEM)
    amps = jnp.transpose(amplitudes, (0, 2, 1, 3)).reshape(864, 384)
    ints = jnp.transpose(cycle_integrals, (0, 2, 1, 3))
    occ_r, virt_r = occ_irrep.reshape(1, 24), virt_irrep.reshape(1, 384)
    params = pltpu.CompilerParams(vmem_limit_bytes=VMEM_LIMIT)
    tsend, wsend, rank = pl.pallas_call(
        pack_kernel,
        out_shape=(
            jax.ShapeDtypeStruct((2, 48, 1152), BF16),
            jax.ShapeDtypeStruct((8, 48, 384), BF16),
            jax.ShapeDtypeStruct((8, 384), F32),
        ),
        in_specs=[vmem, vmem, smem, vmem, vmem],
        out_specs=(vmem, vmem, vmem),
        scratch_shapes=[pltpu.VMEM((3, 864, 128), F32)],
        compiler_params=params,
    )(amps, ints, occ_irrep, occ_r, virt_r)
    dma = pltpu.SemaphoreType.DMA
    resid = pl.pallas_call(
        cycle_kernel,
        out_shape=jax.ShapeDtypeStruct((8, 48, 384), F32),
        in_specs=[vmem, vmem, smem, vmem, vmem, vmem],
        out_specs=vmem,
        scratch_shapes=[
            pltpu.VMEM((2, 8, 48, 384), BF16),
            pltpu.VMEM((8, 2, 48, 1152), BF16),
            pltpu.VMEM((8, 144, 1152), BF16),
            pltpu.VMEM((384, 1152), BF16),
            pltpu.VMEM((8, 1152), I32),
            pltpu.VMEM((2, 8, 48, 384), BF16),
            pltpu.VMEM((8, 48, 384), BF16),
            pltpu.VMEM((8, 48, 384), F32),
            pltpu.VMEM((8, 48, 384), BF16),
            pltpu.VMEM((8, 48, 384), BF16),
            dma, dma, dma, dma, dma, dma, dma((11,)), dma((11,)), dma((11,)), dma((11,)),
            dma((4,)), dma((4,)), dma, dma,
        ],
        compiler_params=pltpu.CompilerParams(
            collective_id=0, has_side_effects=True, vmem_limit_bytes=VMEM_LIMIT
        ),
    )(tsend, wsend, occ_irrep, occ_r, virt_r, rank)
    out = pl.pallas_call(
        update_kernel,
        out_shape=jax.ShapeDtypeStruct((864, 384), F32),
        in_specs=[vmem] * 7,
        out_specs=vmem,
        scratch_shapes=[pltpu.VMEM((3, 864, 128), F32)],
        compiler_params=params,
    )(amps, resid, occ_r, virt_r, rank, occ_energy.reshape(1, 24), virt_energy.reshape(1, 384))
    return jnp.transpose(out.reshape(3, 12, 24, 384), (0, 2, 1, 3))


def solution(mesh):
    return jax.shard_map(
        local,
        mesh=mesh,
        in_specs=(P("occ", None, "virt", None), P("virt", None, "occ", None), P(), P(), P(), P()),
        out_specs=P("occ", None, "virt", None),
        check_vma=False,
    )
```

```python
import jax
import jax.numpy as jnp
from jax import lax
from jax.experimental import pallas as pl
from jax.experimental.pallas import tpu as pltpu
from jax.sharding import PartitionSpec as P

F32, BF16, I32 = jnp.float32, jnp.bfloat16, jnp.int32
MESH = pl.DeviceIdType.MESH
VMEM_LIMIT = 60 << 20


def iota(shape, dim):
    return lax.broadcasted_iota(I32, shape, dim)


def quot(x, d):
    s = 20
    return (x * (-(-(1 << s) // d))) >> s


def parts_of(x, d):
    q = quot(x, d)
    return q, x - q * d


def one_hot(mask):
    return jnp.where(mask, 1.0, 0.0).astype(BF16)


def pick(row, index):
    lanes = iota((index.shape[0], row.shape[1]), 1)
    return jnp.sum(jnp.where(lanes == index, row, 0.0), axis=1, keepdims=True)


def dot_nn(a, b):
    return lax.dot_general(a, b, (((1,), (0,)), ((), ())), preferred_element_type=F32)


def dot_nt(a, b):
    return lax.dot_general(a, b, (((1,), (1,)), ((), ())), preferred_element_type=F32)


def cycle_kernel(
    amps_h, ints_h, occ_s, occ_h, virt_h, occ_eh, virt_eh, out,
    occ_r, virt_r, occ_e, virt_e, gain, expand, diff, amps, ints, rows, tsend, wsend, wstage, tbuf, wring, place, labels, last_rows, gather_last, to_rows, to_owner, rpart, rpeer, dsend, dbuf,
    w_send, w_recv, ws_send, ws_recv, t_send, t_recv, ring_send, ring_recv, sib_send, sib_recv,
    r_send, r_recv, d_send, d_recv, in_sems,
):
    load_ints = pltpu.make_async_copy(ints_h, ints, in_sems.at[0])
    load_amps = pltpu.make_async_copy(amps_h, amps, in_sems.at[1])
    loads = [
        pltpu.make_async_copy(src, dst, in_sems.at[n + 2])
        for n, (src, dst) in enumerate([(occ_h, occ_r), (virt_h, virt_r), (occ_eh, occ_e), (virt_eh, virt_e)])
    ]
    for load in loads:
        load.start()
    load_ints.start()
    load_amps.start()
    o, v = lax.axis_index("occ"), lax.axis_index("virt")
    xh, y = o // 4, lax.rem(o, 4)
    z, s = v // 4, lax.rem(v, 4)
    xl, core = s // 2, lax.rem(s, 2)
    step = 1 - 2 * core
    znext = lax.rem(z + step + 8, 8)
    zback = lax.rem(z - step + 8, 8)

    barrier = pltpu.get_barrier_semaphore()
    for sd in range(4):
        def greet(d, _, sd=sd):
            pl.semaphore_signal(barrier, inc=1, device_id=(lax.rem(o + d, 8), z * 4 + lax.rem(s + sd, 4)), device_id_type=MESH)
            return 0
        lax.fori_loop(1 if sd == 0 else 0, 8, greet, 0)
    for zd in (znext, zback):
        pl.semaphore_signal(barrier, inc=1, device_id=(o, zd * 4 + s), device_id_type=MESH)

    for load in loads:
        load.wait()
    virt = virt_r[...].reshape(1, 384)
    virtf = virt.astype(F32)
    occf = occ_r[...].reshape(1, 24).astype(F32)
    r0, c0 = iota((384, 384), 0), iota((384, 384), 1)
    vcol = jnp.sum(jnp.where(r0 == c0, virtf, 0.0), axis=1, keepdims=True)
    rank = jnp.sum(jnp.where((vcol == virtf) & (r0 < c0), 1.0, 0.0), axis=0, keepdims=True)
    ranki = rank.astype(I32)

    load_ints.wait()
    b, j = parts_of(iota((288, 1), 0), 24)
    label = pick(virtf, v * 12 + b).astype(I32) ^ pick(occf, j).astype(I32)
    total = jnp.zeros((288, 384), F32)
    for k in range(3):
        w = ints[:, k].astype(F32).reshape(288, 384)
        w = jnp.where((label ^ occ_s[3 * o + k]) == virt, w, 0.0).astype(BF16)
        total += dot_nt(w, one_hot(r0 == ranki + (96 * k + 32 * y)))
    od, r = parts_of(iota((384, 1), 0), 48)
    jl, bb = r >> 4, r & 15
    source = jnp.where(bb < 12, bb * 24 + 3 * od + jl, -1)
    wsend[...] = dot_nn(one_hot(iota((384, 288), 1) == source), total.astype(BF16)).astype(BF16).reshape(8, 48, 384)

    pl.semaphore_wait(barrier, 33)

    def w_copy(d):
        od = lax.rem(o + d, 8)
        return pltpu.make_async_remote_copy(
            src_ref=wsend.at[od], dst_ref=wstage.at[core, y * 2 + xl], send_sem=w_send, recv_sem=w_recv,
            device_id=(od, z * 4 + xh * 2 + core), device_id_type=MESH,
        )

    @pl.when(xh == xl)
    def _():
        pltpu.make_async_copy(wsend.at[o], wstage.at[core, y * 2 + xl], w_recv).start()

    @pl.when(xh != xl)
    def _():
        w_copy(0).start()

    def w_start(d, _):
        w_copy(d).start()
        return 0

    lax.fori_loop(1, 8, w_start, 0)

    def t_copy(d, x):
        xd = lax.rem(xl + x, 2)
        return pltpu.make_async_remote_copy(
            src_ref=tsend.at[xd], dst_ref=tbuf.at[o, xl], send_sem=t_send, recv_sem=t_recv,
            device_id=(lax.rem(o + d, 8), z * 4 + xd * 2 + core), device_id_type=MESH,
        )

    load_amps.wait()
    ia, q = parts_of(iota((216, 1), 0), 6)
    i, a = parts_of(ia, 12)
    label = pick(virtf, v * 12 + a).astype(I32) ^ pick(occf, 3 * o + i).astype(I32)
    for lane in range(3):
        rows[lane] = amps[:, lane * 128 : lane * 128 + 128]
    total = jnp.zeros((216, 384), F32)
    for kk in range(4):
        t = jnp.concatenate([rows[lane, pl.ds(kk, 216, stride=4), :] for lane in range(3)], axis=1)
        t = jnp.where((label ^ pick(occf, 4 * q + kk).astype(I32)) == virt, t, 0.0).astype(BF16)
        total += dot_nt(t, one_hot(r0 == ranki + 96 * kk))
    qd, r = parts_of(iota((288, 1), 0), 48)
    source = jnp.where(r < 36, r * 6 + qd, -1)
    t = dot_nn(one_hot(iota((288, 216), 1) == source), total.astype(BF16))
    last_rows[...] = jnp.zeros((2, 48, 128), F32)
    for q in range(6):
        for lane in range(3):
            tile = t[q * 48 : q * 48 + 36, lane * 128 : lane * 128 + 128]
            n = (q % 3) * 3 + lane
            tsend[q // 3, n * 32 : n * 32 + 32] = tile[0:32].astype(BF16)
            last_rows[q // 3, n * 4 : n * 4 + 4] = tile[32:36]
    tsend[:, 288:336] = last_rows[...].astype(BF16)

    n = iota((144, 1), 0)
    gather_last[...] = one_hot(iota((144, 192), 1) == ((n & 15) >> 2) * 48 + (n >> 4) * 4 + (n & 3))
    n = iota((160, 1), 0)
    x, n = parts_of(n, 80)
    u, r = parts_of(n, 36)
    block = u * 2 + x
    source = jnp.where(u < 2, jnp.where(r < 32, block * 32 + r, 96 + block * 4 + r), -1)
    to_rows[...] = one_hot(iota((160, 144), 1) == source)
    u, r = parts_of(iota((96, 1), 0), 48)
    i, a = r >> 4, r & 15
    to_owner[...] = one_hot(iota((96, 80), 1) == jnp.where(a < 12, u * 36 + i * 12 + a, -1))

    n = iota((1, 1152), 1)
    zz, r = parts_of(n, 144)
    jl, b48 = parts_of(r, 48)
    values = jnp.concatenate([jnp.broadcast_to(rank, (4, 384)), jnp.broadcast_to(virtf, (4, 384))], axis=0)
    spread = dot_nn(values.astype(BF16), one_hot(iota((384, 1152), 0) == zz * 48 + b48)).astype(I32)
    place[...] = one_hot(iota((384, 1152), 0) == spread[0:1, :] + jl * 128)
    oj = jnp.where(jl == 0, occ_s[3 * o], jnp.where(jl == 1, occ_s[3 * o + 1], occ_s[3 * o + 2]))
    labels[...] = jnp.broadcast_to(spread[4:5, :] ^ oj, (8, 1152))

    row = iota((144, 1), 0)
    jr, br = parts_of(row, 48)
    sr, bl = parts_of(br, 12)
    gather = one_hot(iota((144, 192), 1) == (sr & 1) * 96 + (sr >> 1) * 48 + jr * 16 + bl)
    w_share = pltpu.make_async_remote_copy(
        src_ref=wstage.at[core], dst_ref=wstage.at[core], send_sem=ws_send, recv_sem=ws_recv,
        device_id=(o, z * 4 + xl * 2 + 1 - core), device_id_type=MESH,
    )
    pltpu.make_async_copy(wstage.at[core], wstage.at[core], w_recv).wait()
    w_share.start()
    pltpu.make_async_copy(tsend.at[xl], tbuf.at[o, xl], t_recv).start()
    for n in range(15):
        t_copy((n + 1) // 2, (n + 1) % 2).start()
    pltpu.make_async_copy(wstage.at[1 - core], wstage.at[1 - core], ws_recv).wait()
    last = None
    for yy in range(4):
        piece = dot_nn(gather, wstage[:, yy * 2 : yy * 2 + 2].reshape(192, 384))
        first = piece[:, 0:128] if last is None else piece[:, 0:128] + last
        wring[z, :, yy * 256 : yy * 256 + 128] = first.astype(BF16)
        wring[z, :, yy * 256 + 128 : yy * 256 + 256] = piece[:, 128:256].astype(BF16)
        last = piece[:, 256:384]
    wring[z, :, 1024:1152] = last.astype(BF16)

    def piece_of(block, start, size):
        return wring.at[lax.rem(block + 8, 8), pl.ds(pl.multiple_of(start, 16), size)]

    def first_row(g, c):
        return 48 * g + c * (96 - 96 * g)

    def ring_copy(t, g, start, size=48):
        ref = piece_of(z - step * (t - 1), start, size)
        n = 3 * t - 3 + g
        return pltpu.make_async_remote_copy(
            src_ref=ref, dst_ref=ref, send_sem=ring_send.at[n], recv_sem=ring_recv.at[n],
            device_id=(o, znext * 4 + s), device_id_type=MESH,
        )

    def sib_copy(t, g, start, size=48):
        ref = piece_of(z - step * t, start, size)
        n = 3 * t - 3 + g
        return pltpu.make_async_remote_copy(
            src_ref=ref, dst_ref=ref, send_sem=sib_send.at[n], recv_sem=sib_recv.at[n],
            device_id=(o, z * 4 + xl * 2 + 1 - core), device_id_type=MESH,
        )

    def arrived(t, g, sems, way, start, size=48):
        ref = piece_of(z - way * t, start, size)
        pltpu.make_async_copy(ref, ref, sems.at[3 * t - 3 + g]).wait()

    rest = ((48, 32), (80, 16))
    for g in range(3):
        ring_copy(1, g, first_row(g, core)).start()

    expand[...] = one_hot((iota((256, 384), 0) & 127) == ranki)
    occ_en, virt_en = occ_e[...].reshape(1, 24), virt_e[...].reshape(1, 384)
    for i in range(3):
        a, j = parts_of(iota((288, 1), 0), 24)
        at = pl.ds(i * 288, 288)
        own = jnp.full((288, 1), 3 * o + i)
        label = pick(virtf, v * 12 + a).astype(I32) ^ pick(occf, j).astype(I32) ^ pick(occf, own).astype(I32)
        denom = pick(occ_en, own) + pick(occ_en, j) - pick(virt_en, v * 12 + a) - virt_en
        gain[at, :] = jnp.where(label == virt, 1.0 / denom, 0.0)
        amps[at, :] = jnp.where(label == virt, amps[at, :], 0.0)

    for t in range(1, 4):
        for g in range(3):
            start = first_row(g, core)
            arrived(t, g, ring_recv, step, start)
            if t < 3 or g == 0:
                ring_copy(t + 1, g, start).start()
            elif g == 1:
                for c in range(2):
                    @pl.when(core == c)
                    def _(c=c):
                        ring_copy(4, 1, *rest[c]).start()
            sib_copy(t, g, start).start()
    arrived(4, 0, ring_recv, step, first_row(0, core))
    sib_copy(4, 0, first_row(0, core)).start()
    for c in range(2):
        @pl.when(core == c)
        def _(c=c):
            arrived(4, 1, ring_recv, step, *rest[c])
            sib_copy(4, 1, *rest[c]).start()
            arrived(4, 1, sib_recv, -step, *rest[1 - c])
    for t in range(1, 5):
        for g in range(3 if t < 4 else 1):
            arrived(t, g, sib_recv, -step, first_row(g, 1 - core))

    pltpu.make_async_copy(tbuf, tbuf, t_recv).wait()


    def r_copy(c):
        p = lax.rem(o // 2 + c, 4)
        return pltpu.make_async_remote_copy(
            src_ref=rpart.at[1 - xl, p], dst_ref=rpeer.at[p],
            send_sem=r_send.at[c], recv_sem=r_recv.at[c],
            device_id=(o, z * 4 + (1 - xl) * 2 + core), device_id_type=MESH,
        )

    def product(c, _):
        p = lax.rem(o // 2 + c, 4)
        tiles = tbuf[pl.ds(2 * p, 2)].reshape(4, 336, 128)
        last = dot_nn(gather_last[...], tiles[:, 288:336].reshape(192, 128)).astype(BF16)
        left = jnp.concatenate(
            [
                jnp.concatenate([tiles[:, n * 32 : n * 32 + 32].reshape(128, 128), last[n * 16 : n * 16 + 16]], axis=0)
                for n in range(9)
            ],
            axis=1,
        )
        n = iota((144, 1), 0)
        block = jnp.where(n < 128, n >> 5, (n - 128) >> 2)
        il, a = parts_of(jnp.where(n < 128, n & 31, 32 + (n & 3)), 12)
        a = z * 48 + (block & 1) * 24 + core * 12 + a
        i = 6 * p + 3 * (block >> 1) + il
        label = pick(virtf, a).astype(I32) ^ pick(occf, i).astype(I32)
        raw = dot_nt(left, wring[...].reshape(1152, 1152))
        raw = jnp.where(label == labels[0:1, :], raw, 0.0).astype(BF16)
        packed = dot_nn(to_rows[...], dot_nt(raw, place[...]).astype(BF16)).astype(BF16)
        rpart[0, p] = packed[0:80]
        rpart[1, p] = packed[80:160]
        r_copy(c).start()
        return 0

    lax.fori_loop(0, 4, product, 0)

    def d_copy(od):
        return pltpu.make_async_remote_copy(
            src_ref=dsend.at[od], dst_ref=dbuf.at[o], send_sem=d_send, recv_sem=d_recv,
            device_id=(od, v), device_id_type=MESH,
        )

    d_local = pltpu.make_async_copy(dsend.at[o], dbuf.at[o], d_recv)

    def combine(c, _):
        p = lax.rem(o // 2 + c, 4)
        r_copy(c).wait_recv()
        both = rpart[xl, p].astype(F32) + rpeer[p].astype(F32)
        dsend[pl.ds(2 * p, 2)] = dot_nn(to_owner[...], both.astype(BF16)).astype(BF16).reshape(2, 48, 384)
        for u in range(2):
            od = 2 * p + u

            @pl.when(od == o)
            def _():
                d_local.start()

            @pl.when(od != o)
            def _(od=od):
                d_copy(od).start()
        return 0

    lax.fori_loop(0, 4, combine, 0)
    pltpu.make_async_copy(dbuf, dbuf, d_recv).wait()

    def differ(g, _):
        for jl in range(3):
            direct = dbuf[g, :, jl * 128 : jl * 128 + 128].astype(F32)
            for i in range(3):
                change = direct[i * 16 : i * 16 + 16] - dsend[g, jl * 16 : jl * 16 + 16, i * 128 : i * 128 + 128].astype(F32)
                high = change.astype(BF16)
                diff[i, 3 * g + jl, :, 0:128] = high
                diff[i, 3 * g + jl, :, 128:256] = (change - high.astype(F32)).astype(BF16)
        return 0

    lax.fori_loop(0, 8, differ, 0)
    stores = []
    for i in range(3):
        at = pl.ds(i * 288, 288)
        e = dot_nn(diff[i].reshape(384, 256), expand[...])
        for j in range(24):
            for lane in range(3):
                rows[lane, pl.ds(i * 288 + j, 12, stride=24), :] = e[j * 16 : j * 16 + 12, lane * 128 : lane * 128 + 128]
        for lane in range(3):
            to = slice(lane * 128, lane * 128 + 128)
            amps[at, to] = amps[at, to] + rows[lane, at, :] * gain[at, to]
        stores.append(pltpu.make_async_copy(amps.at[at], out.at[at], in_sems.at[i]))
        stores[i].start()

    @pl.when(xh != xl)
    def _():
        w_copy(0).wait_send()

    def sent(d, _):
        w_copy(d).wait_send()
        t_copy(d, 0).wait_send()
        t_copy(d, 1).wait_send()
        d_copy(lax.rem(o + d, 8)).wait_send()
        return 0

    lax.fori_loop(1, 8, sent, 0)
    t_copy(0, 1).wait_send()
    w_share.wait_send()
    for t in range(1, 5):
        for g in range(3 if t < 4 else 1):
            ring_copy(t, g, first_row(g, core)).wait_send()
            sib_copy(t, g, first_row(g, core)).wait_send()
    for c in range(2):
        @pl.when(core == c)
        def _(c=c):
            ring_copy(4, 1, *rest[c]).wait_send()
            sib_copy(4, 1, *rest[c]).wait_send()
    for c in range(4):
        r_copy(c).wait_send()
    for store in stores:
        store.wait()


def local(amplitudes, cycle_integrals, occ_energy, virt_energy, occ_irrep, virt_irrep):
    smem = pl.BlockSpec(memory_space=pltpu.SMEM)
    amps = jnp.transpose(amplitudes, (0, 2, 1, 3)).reshape(864, 384)
    ints = jnp.transpose(cycle_integrals, (0, 2, 1, 3))
    dma = pltpu.SemaphoreType.DMA
    hbm = pl.BlockSpec(memory_space=pltpu.HBM)
    out = pl.pallas_call(
        cycle_kernel,
        out_shape=jax.ShapeDtypeStruct((864, 384), F32),
        in_specs=[hbm, hbm, smem, hbm, hbm, hbm, hbm],
        out_specs=hbm,
        scratch_shapes=[
            pltpu.VMEM((24,), I32),
            pltpu.VMEM((384,), I32),
            pltpu.VMEM((24,), F32),
            pltpu.VMEM((384,), F32),
            pltpu.VMEM((864, 384), F32),
            pltpu.VMEM((256, 384), BF16),
            pltpu.VMEM((3, 24, 16, 256), BF16),
            pltpu.VMEM((864, 384), F32),
            pltpu.VMEM((12, 3, 24, 384), BF16),
            pltpu.VMEM((3, 864, 128), F32),
            pltpu.VMEM((2, 336, 128), BF16),
            pltpu.VMEM((8, 48, 384), BF16),
            pltpu.VMEM((2, 8, 48, 384), BF16),
            pltpu.VMEM((8, 2, 336, 128), BF16),
            pltpu.VMEM((8, 144, 1152), BF16),
            pltpu.VMEM((384, 1152), BF16),
            pltpu.VMEM((8, 1152), I32),
            pltpu.VMEM((2, 48, 128), F32),
            pltpu.VMEM((144, 192), BF16),
            pltpu.VMEM((160, 144), BF16),
            pltpu.VMEM((96, 80), BF16),
            pltpu.VMEM((2, 4, 80, 384), BF16),
            pltpu.VMEM((4, 80, 384), BF16),
            pltpu.VMEM((8, 48, 384), BF16),
            pltpu.VMEM((8, 48, 384), BF16),
            dma, dma, dma, dma, dma, dma, dma((11,)), dma((11,)), dma((11,)), dma((11,)),
            dma((4,)), dma((4,)), dma, dma, dma((6,)),
        ],
        compiler_params=pltpu.CompilerParams(
            collective_id=0, has_side_effects=True, vmem_limit_bytes=VMEM_LIMIT
        ),
    )(amps, ints, occ_irrep, occ_irrep, virt_irrep, occ_energy, virt_energy)
    return jnp.transpose(out.reshape(3, 12, 24, 384), (0, 2, 1, 3))


def solution(mesh):
    return jax.shard_map(
        local,
        mesh=mesh,
        in_specs=(P("occ", None, "virt", None), P("virt", None, "occ", None), P(), P(), P(), P()),
        out_specs=P("occ", None, "virt", None),
        check_vma=False,
    )
```

```python
import jax
import jax.numpy as jnp
from jax import lax
from jax.experimental import pallas as pl
from jax.experimental.pallas import tpu as pltpu
from jax.sharding import PartitionSpec as P

F32, BF16, I32 = jnp.float32, jnp.bfloat16, jnp.int32
MESH = pl.DeviceIdType.MESH
VMEM_LIMIT = 60 << 20


def iota(shape, dim):
    return lax.broadcasted_iota(I32, shape, dim)


def quot(x, d):
    s = 20
    return (x * (-(-(1 << s) // d))) >> s


def parts_of(x, d):
    q = quot(x, d)
    return q, x - q * d


def one_hot(mask):
    return jnp.where(mask, 1.0, 0.0).astype(BF16)


def pick(row, index):
    lanes = iota((index.shape[0], row.shape[1]), 1)
    return jnp.sum(jnp.where(lanes == index, row, 0.0), axis=1, keepdims=True)


def dot_nn(a, b):
    return lax.dot_general(a, b, (((1,), (0,)), ((), ())), preferred_element_type=F32)


def dot_nt(a, b):
    return lax.dot_general(a, b, (((1,), (1,)), ((), ())), preferred_element_type=F32)


def cycle_kernel(
    amps_h, ints_h, occ_s, occ_h, virt_h, occ_eh, virt_eh, out,
    occ_r, virt_r, occ_e, virt_e, gain, expand, diff, amps, ints, rows, tsend, w_last, wsend, wstage, tbuf, wring, place, labels, last_rows, gather_last, to_rows, to_owner, row_labels,
    left, rpart, rpeer, dsend, dbuf,
    w_send, w_recv, t_send, t_recv, ring_send, ring_recv, sib_send, sib_recv,
    r_send, r_recv, d_send, d_recv, in_sems,
):
    load_ints = pltpu.make_async_copy(ints_h, ints, in_sems.at[0])
    load_amps = pltpu.make_async_copy(amps_h, amps, in_sems.at[1])
    loads = [
        pltpu.make_async_copy(src, dst, in_sems.at[n + 2])
        for n, (src, dst) in enumerate([(occ_h, occ_r), (virt_h, virt_r), (occ_eh, occ_e), (virt_eh, virt_e)])
    ]
    for load in loads:
        load.start()
    load_ints.start()
    load_amps.start()
    o, v = lax.axis_index("occ"), lax.axis_index("virt")
    xh, y = o // 4, lax.rem(o, 4)
    z, s = v // 4, lax.rem(v, 4)
    xl, core = s // 2, lax.rem(s, 2)

    barrier = pltpu.get_barrier_semaphore()
    for sd in range(4):
        def greet(d, _, sd=sd):
            pl.semaphore_signal(barrier, inc=1, device_id=(lax.rem(o + d, 8), z * 4 + lax.rem(s + sd, 4)), device_id_type=MESH)
            return 0
        lax.fori_loop(1 if sd == 0 else 0, 8, greet, 0)
    for zd in (lax.rem(z + 1, 8), lax.rem(z + 7, 8)):
        pl.semaphore_signal(barrier, inc=1, device_id=(o, zd * 4 + s), device_id_type=MESH)

    for load in loads:
        load.wait()
    virt = virt_r[...].reshape(1, 384)
    virtf = virt.astype(F32)
    occf = occ_r[...].reshape(1, 24).astype(F32)
    r0, c0 = iota((384, 384), 0), iota((384, 384), 1)
    vcol = jnp.sum(jnp.where(r0 == c0, virtf, 0.0), axis=1, keepdims=True)
    rank = jnp.sum(jnp.where((vcol == virtf) & (r0 < c0), 1.0, 0.0), axis=0, keepdims=True)
    ranki = rank.astype(I32)

    load_ints.wait()
    b, j = parts_of(iota((288, 1), 0), 24)
    label = pick(virtf, v * 12 + b).astype(I32) ^ pick(occf, j).astype(I32)
    total = jnp.zeros((288, 384), F32)
    for k in range(3):
        w = ints[:, k].astype(F32).reshape(288, 384)
        w = jnp.where((label ^ occ_s[3 * o + k]) == virt, w, 0.0).astype(BF16)
        total += dot_nt(w, one_hot(r0 == ranki + (96 * k + 32 * y)))
    od, r = parts_of(iota((384, 1), 0), 48)
    jl, b = parts_of(r, 12)
    source = jnp.where(r < 36, b * 24 + 3 * od + jl, -1)
    w = dot_nn(one_hot(iota((384, 288), 1) == source), total.astype(BF16))
    w_last[...] = jnp.zeros((8, 16, 128), F32)
    for d in range(8):
        for n in range(3):
            tile = w[d * 48 : d * 48 + 36, n * 128 : n * 128 + 128]
            wsend[d, n * 32 : n * 32 + 32] = tile[0:32].astype(BF16)
            w_last[d, n * 4 : n * 4 + 4] = tile[32:36]
    wsend[:, 96:112] = w_last[...].astype(BF16)

    pl.semaphore_wait(barrier, 33)

    def w_copy(d):
        od = lax.rem(o + d, 8)
        return pltpu.make_async_remote_copy(
            src_ref=wsend.at[od], dst_ref=wstage.at[y * 2 + xl], send_sem=w_send, recv_sem=w_recv,
            device_id=(od, z * 4 + xh * 2 + core), device_id_type=MESH,
        )

    @pl.when(xh == xl)
    def _():
        pltpu.make_async_copy(wsend.at[o], wstage.at[y * 2 + xl], w_recv).start()

    @pl.when(xh != xl)
    def _():
        w_copy(0).start()

    def w_start(d, _):
        w_copy(d).start()
        return 0

    lax.fori_loop(1, 8, w_start, 0)

    def t_copy(d, x):
        xd = lax.rem(xl + x, 2)
        return pltpu.make_async_remote_copy(
            src_ref=tsend.at[xd], dst_ref=tbuf.at[o, xl], send_sem=t_send, recv_sem=t_recv,
            device_id=(lax.rem(o + d, 8), z * 4 + xd * 2 + core), device_id_type=MESH,
        )

    load_amps.wait()
    ia, q = parts_of(iota((216, 1), 0), 6)
    i, a = parts_of(ia, 12)
    label = pick(virtf, v * 12 + a).astype(I32) ^ pick(occf, 3 * o + i).astype(I32)
    for lane in range(3):
        rows[lane] = amps[:, lane * 128 : lane * 128 + 128]
    total = jnp.zeros((216, 384), F32)
    for kk in range(4):
        t = jnp.concatenate([rows[lane, pl.ds(kk, 216, stride=4), :] for lane in range(3)], axis=1)
        t = jnp.where((label ^ pick(occf, 4 * q + kk).astype(I32)) == virt, t, 0.0).astype(BF16)
        total += dot_nt(t, one_hot(r0 == ranki + 96 * kk))
    qd, r = parts_of(iota((288, 1), 0), 48)
    source = jnp.where(r < 36, r * 6 + qd, -1)
    t = dot_nn(one_hot(iota((288, 216), 1) == source), total.astype(BF16))
    last_rows[...] = jnp.zeros((2, 48, 128), F32)
    for q in range(6):
        for lane in range(3):
            tile = t[q * 48 : q * 48 + 36, lane * 128 : lane * 128 + 128]
            n = (q % 3) * 3 + lane
            tsend[q // 3, n * 32 : n * 32 + 32] = tile[0:32].astype(BF16)
            last_rows[q // 3, n * 4 : n * 4 + 4] = tile[32:36]
    tsend[:, 288:336] = last_rows[...].astype(BF16)

    n = iota((288, 1), 0)
    gather_last[...] = one_hot(iota((288, 384), 1) == ((n & 31) >> 2) * 48 + (n >> 5) * 4 + (n & 3))
    x, n = parts_of(n, 144)
    u, r = parts_of(n, 36)
    block = u * 2 + x
    to_rows[...] = one_hot(iota((288, 288), 1) == jnp.where(r < 32, block * 32 + r, 224 + block * 4 + r))
    u, r = parts_of(iota((192, 1), 0), 48)
    i, a = r >> 4, r & 15
    to_owner[...] = one_hot(iota((192, 144), 1) == jnp.where(a < 12, u * 36 + i * 12 + a, -1))

    values = jnp.concatenate([jnp.broadcast_to(rank, (4, 384)), jnp.broadcast_to(virtf, (4, 384))], axis=0).astype(BF16)
    zz, r = parts_of(iota((1, 1280), 1), 160)
    c, r = parts_of(r, 80)
    x = jnp.where(r < 64, r >> 5, (r - 64) >> 2)
    jl, bl = parts_of(jnp.where(r < 64, r & 31, 32 + (r & 3)), 12)
    b = ((z + zz + 6) & 7) * 48 + x * 24 + c * 12 + bl
    spread = dot_nn(values, one_hot(iota((384, 1280), 0) == b)).astype(I32)
    place[...] = one_hot(iota((384, 1280), 0) == spread[0:1, :] + jl * 128)
    oj = jnp.where(jl == 0, occ_s[3 * o], jnp.where(jl == 1, occ_s[3 * o + 1], occ_s[3 * o + 2]))
    labels[...] = jnp.broadcast_to(jnp.where(r < 72, spread[4:5, :] ^ oj, -1), (8, 1280))

    x, n = parts_of(iota((288, 1), 0), 144)
    u, r = parts_of(n, 36)
    il, a = parts_of(r, 12)
    label = pick(virtf, z * 48 + x * 24 + core * 12 + a).astype(I32)
    for half in range(2):
        own = label ^ pick(occf, 12 * half + 3 * u + il).astype(I32)
        row_labels[half] = jnp.broadcast_to(own, (288, 128))

    expand[...] = one_hot((iota((256, 384), 0) & 127) == ranki)
    occ_en, virt_en = occ_e[...].reshape(1, 24), virt_e[...].reshape(1, 384)
    for i in range(3):
        a, j = parts_of(iota((288, 1), 0), 24)
        at = pl.ds(i * 288, 288)
        own = jnp.full((288, 1), 3 * o + i)
        label = pick(virtf, v * 12 + a).astype(I32) ^ pick(occf, j).astype(I32) ^ pick(occf, own).astype(I32)
        denom = pick(occ_en, own) + pick(occ_en, j) - pick(virt_en, v * 12 + a) - virt_en
        gain[at, :] = jnp.where(label == virt, 1.0 / denom, 0.0)
        amps[at, :] = jnp.where(label == virt, amps[at, :], 0.0)

    n = iota((96, 1), 0)
    zz, r = parts_of(n, 24)
    gather = one_hot(iota((96, 128), 1) == (zz * 2 + ((r & 7) >> 2)) * 16 + (r >> 3) * 4 + (r & 3))
    pltpu.make_async_copy(wstage, wstage, w_recv).wait()
    tails = dot_nn(gather, wstage[:, 96:112].reshape(128, 128))
    last = None
    zero = jnp.zeros((8, 128), F32)
    for yy in range(4):
        piece = []
        for n in range(3):
            main = wstage[yy * 2 : yy * 2 + 2, n * 32 : n * 32 + 32].reshape(64, 128).astype(F32)
            at = yy * 24 + n * 8
            piece.append(jnp.concatenate([main, tails[at : at + 8], zero], axis=0))
        first = piece[0] if last is None else piece[0] + last
        wring[2, core, :, yy * 256 : yy * 256 + 128] = first.astype(BF16)
        wring[2, core, :, yy * 256 + 128 : yy * 256 + 256] = piece[1].astype(BF16)
        last = piece[2]
    wring[2, core, :, 1024:1152] = last.astype(BF16)

    def half_block(way, t, c):
        return wring.at[(2 - way * t) % 8, c]

    def piece_of(way, t, g):
        return wring.at[(2 - way * t) % 8, core, pl.ds(pl.multiple_of(16 * g, 16), 16)]

    def ring_copy(way, t, g):
        w = (1 - way) // 2
        return pltpu.make_async_remote_copy(
            src_ref=piece_of(way, t - 1, g), dst_ref=piece_of(way, t, g),
            send_sem=ring_send.at[w * 4 + t - 1], recv_sem=ring_recv.at[w * 20 + 5 * t - 5 + g],
            device_id=(o, lax.rem(z + way + 8, 8) * 4 + s), device_id_type=MESH,
        )

    def ring_arrived(way, t, g):
        ref = piece_of(way, t, g)
        pltpu.make_async_copy(ref, ref, ring_recv.at[(1 - way) // 2 * 20 + 5 * t - 5 + g]).wait()

    def to_sibling(ref, n):
        return pltpu.make_async_remote_copy(
            src_ref=ref, dst_ref=ref, send_sem=sib_send.at[n], recv_sem=sib_recv.at[n],
            device_id=(o, z * 4 + xl * 2 + 1 - core), device_id_type=MESH,
        )

    def sib_copy(way, t, g):
        return to_sibling(piece_of(way, t, g), (1 - way) // 2 * 3 + t if t < 4 else 7)

    def sib_arrived(ref, n):
        pltpu.make_async_copy(ref, ref, sib_recv.at[n]).wait()

    def each(count, body):
        def run(g, _):
            body(g)
            return 0
        lax.fori_loop(0, count, run, 0)

    def begin(g):
        ring_copy(1, 1, g).start()
        ring_copy(-1, 1, g).start()

    each(5, begin)
    to_sibling(wring.at[2, core], 0).start()
    pltpu.make_async_copy(tsend.at[xl], tbuf.at[o, xl], t_recv).start()
    for n in range(15):
        t_copy((n + 1) // 2, (n + 1) % 2).start()
    for t in range(1, 4):
        def pass_on(g, t=t):
            for way in (1, -1):
                ring_arrived(way, t, g)
                if t < 3:
                    ring_copy(way, t + 1, g).start()
                else:
                    @pl.when(core == (1 - way) // 2)
                    def _(way=way):
                        ring_copy(way, 4, g).start()
                sib_copy(way, t, g).start()

        each(5, pass_on)

    pltpu.make_async_copy(tbuf, tbuf, t_recv).wait()

    def near(half, _):
        tiles = tbuf[pl.ds(4 * half, 4)].reshape(8, 336, 128)
        last = dot_nn(gather_last[...], tiles[:, 288:336].reshape(384, 128)).astype(BF16)
        rows36 = jnp.concatenate(
            [
                jnp.concatenate([tiles[:, n * 32 : n * 32 + 32].reshape(256, 128), last[n * 32 : n * 32 + 32]], axis=0)
                for n in range(9)
            ],
            axis=1,
        )
        left[half] = dot_nn(to_rows[...], rows36).astype(BF16)
        return 0

    lax.fori_loop(0, 2, near, 0)

    for way in (1, -1):
        @pl.when(core == (1 - way) // 2)
        def _(way=way):
            def keep(g):
                ring_arrived(way, 4, g)
                sib_copy(way, 4, g).start()

            each(5, keep)
    sib_arrived(wring.at[2, 1 - core], 0)
    for way in (1, -1):
        for t in range(1, 4):
            sib_arrived(half_block(way, t, 1 - core), (1 - way) // 2 * 3 + t)
    sib_arrived(half_block(1, 4, 1 - core), 7)

    def r_copy(c):
        half = lax.rem(xh + 1 + c, 2)
        return pltpu.make_async_remote_copy(
            src_ref=rpart.at[1 - xl, half], dst_ref=rpeer.at[half],
            send_sem=r_send.at[c], recv_sem=r_recv.at[c],
            device_id=(o, z * 4 + (1 - xl) * 2 + core), device_id_type=MESH,
        )

    def product(c, _):
        half = lax.rem(xh + 1 + c, 2)
        raw = dot_nt(left[half], wring[...].reshape(1280, 1152))
        raw = jnp.where(row_labels[half][:, 0:1] == labels[0:1, :], raw, 0.0).astype(BF16)
        both = dot_nt(raw, place[...]).astype(BF16)
        rpart[0, half] = both[0:144]
        rpart[1, half] = both[144:288]
        r_copy(c).start()
        return 0

    lax.fori_loop(0, 2, product, 0)

    def d_copy(od):
        return pltpu.make_async_remote_copy(
            src_ref=dsend.at[od], dst_ref=dbuf.at[o], send_sem=d_send, recv_sem=d_recv,
            device_id=(od, v), device_id_type=MESH,
        )

    d_local = pltpu.make_async_copy(dsend.at[o], dbuf.at[o], d_recv)

    def combine(c, _):
        half = lax.rem(xh + 1 + c, 2)
        r_copy(c).wait_recv()
        both = rpart[xl, half].astype(F32) + rpeer[half].astype(F32)
        dsend[pl.ds(4 * half, 4)] = dot_nn(to_owner[...], both.astype(BF16)).astype(BF16).reshape(4, 48, 384)
        for u in range(4):
            od = 4 * half + lax.rem(y + 1 + u, 4)

            @pl.when(od == o)
            def _():
                d_local.start()

            @pl.when(od != o)
            def _(od=od):
                d_copy(od).start()
        return 0

    lax.fori_loop(0, 2, combine, 0)
    pltpu.make_async_copy(dbuf, dbuf, d_recv).wait()

    def differ(g, _):
        for jl in range(3):
            direct = dbuf[g, :, jl * 128 : jl * 128 + 128].astype(F32)
            for i in range(3):
                change = direct[i * 16 : i * 16 + 16] - dsend[g, jl * 16 : jl * 16 + 16, i * 128 : i * 128 + 128].astype(F32)
                high = change.astype(BF16)
                diff[i, 3 * g + jl, :, 0:128] = high
                diff[i, 3 * g + jl, :, 128:256] = (change - high.astype(F32)).astype(BF16)
        return 0

    lax.fori_loop(0, 8, differ, 0)
    stores = []
    for i in range(3):
        at = pl.ds(i * 288, 288)
        e = dot_nn(diff[i].reshape(384, 256), expand[...])
        for j in range(24):
            for lane in range(3):
                rows[lane, pl.ds(i * 288 + j, 12, stride=24), :] = e[j * 16 : j * 16 + 12, lane * 128 : lane * 128 + 128]
        for lane in range(3):
            to = slice(lane * 128, lane * 128 + 128)
            amps[at, to] = amps[at, to] + rows[lane, at, :] * gain[at, to]
        stores.append(pltpu.make_async_copy(amps.at[at], out.at[at], in_sems.at[i]))
        stores[i].start()

    @pl.when(xh != xl)
    def _():
        w_copy(0).wait_send()

    def sent(d, _):
        w_copy(d).wait_send()
        t_copy(d, 0).wait_send()
        t_copy(d, 1).wait_send()
        d_copy(lax.rem(o + d, 8)).wait_send()
        return 0

    lax.fori_loop(1, 8, sent, 0)
    t_copy(0, 1).wait_send()
    to_sibling(wring.at[2, core], 0).wait_send()
    for way in (1, -1):
        for t in range(1, 4):
            def left_here(g, way=way, t=t):
                ring_copy(way, t, g).wait_send()
                sib_copy(way, t, g).wait_send()

            each(5, left_here)

        @pl.when(core == (1 - way) // 2)
        def _(way=way):
            def far_left(g):
                ring_copy(way, 4, g).wait_send()
                sib_copy(way, 4, g).wait_send()

            each(5, far_left)

    for c in range(2):
        r_copy(c).wait_send()
    for store in stores:
        store.wait()


def local(amplitudes, cycle_integrals, occ_energy, virt_energy, occ_irrep, virt_irrep):
    smem = pl.BlockSpec(memory_space=pltpu.SMEM)
    amps = jnp.transpose(amplitudes, (0, 2, 1, 3)).reshape(864, 384)
    ints = jnp.transpose(cycle_integrals, (0, 2, 1, 3))
    dma = pltpu.SemaphoreType.DMA
    hbm = pl.BlockSpec(memory_space=pltpu.HBM)
    out = pl.pallas_call(
        cycle_kernel,
        out_shape=jax.ShapeDtypeStruct((864, 384), F32),
        in_specs=[hbm, hbm, smem, hbm, hbm, hbm, hbm],
        out_specs=hbm,
        scratch_shapes=[
            pltpu.VMEM((24,), I32),
            pltpu.VMEM((384,), I32),
            pltpu.VMEM((24,), F32),
            pltpu.VMEM((384,), F32),
            pltpu.VMEM((864, 384), F32),
            pltpu.VMEM((256, 384), BF16),
            pltpu.VMEM((3, 24, 16, 256), BF16),
            pltpu.VMEM((864, 384), F32),
            pltpu.VMEM((12, 3, 24, 384), BF16),
            pltpu.VMEM((3, 864, 128), F32),
            pltpu.VMEM((2, 336, 128), BF16),
            pltpu.VMEM((8, 16, 128), F32),
            pltpu.VMEM((8, 112, 128), BF16),
            pltpu.VMEM((8, 112, 128), BF16),
            pltpu.VMEM((8, 2, 336, 128), BF16),
            pltpu.VMEM((8, 2, 80, 1152), BF16),
            pltpu.VMEM((384, 1280), BF16),
            pltpu.VMEM((8, 1280), I32),
            pltpu.VMEM((2, 48, 128), F32),
            pltpu.VMEM((288, 384), BF16),
            pltpu.VMEM((288, 288), BF16),
            pltpu.VMEM((192, 144), BF16),
            pltpu.VMEM((2, 288, 128), I32),
            pltpu.VMEM((2, 288, 1152), BF16),
            pltpu.VMEM((2, 2, 144, 384), BF16),
            pltpu.VMEM((2, 144, 384), BF16),
            pltpu.VMEM((8, 48, 384), BF16),
            pltpu.VMEM((8, 48, 384), BF16),
            dma, dma, dma, dma, dma((8,)), dma((40,)), dma((8,)), dma((8,)),
            dma((2,)), dma((2,)), dma, dma, dma((6,)),
        ],
        compiler_params=pltpu.CompilerParams(
            collective_id=0, has_side_effects=True, vmem_limit_bytes=VMEM_LIMIT
        ),
    )(amps, ints, occ_irrep, occ_irrep, virt_irrep, occ_energy, virt_energy)
    return jnp.transpose(out.reshape(3, 12, 24, 384), (0, 2, 1, 3))


def solution(mesh):
    return jax.shard_map(
        local,
        mesh=mesh,
        in_specs=(P("occ", None, "virt", None), P("virt", None, "occ", None), P(), P(), P(), P()),
        out_specs=P("occ", None, "virt", None),
        check_vma=False,
    )
```

```python
import jax
import jax.numpy as jnp
from jax import lax
from jax.experimental import pallas as pl
from jax.experimental.pallas import tpu as pltpu
from jax.sharding import PartitionSpec as P

F32, BF16, I32 = jnp.float32, jnp.bfloat16, jnp.int32
MESH = pl.DeviceIdType.MESH
VMEM_LIMIT = 60 << 20


def iota(shape, dim):
    return lax.broadcasted_iota(I32, shape, dim)


def quot(x, d):
    s = 20
    return (x * (-(-(1 << s) // d))) >> s


def parts_of(x, d):
    q = quot(x, d)
    return q, x - q * d


def one_hot(mask):
    return jnp.where(mask, 1.0, 0.0).astype(BF16)


def pick(row, index):
    lanes = iota((index.shape[0], row.shape[1]), 1)
    return jnp.sum(jnp.where(lanes == index, row, 0.0), axis=1, keepdims=True)


def dot_nn(a, b):
    return lax.dot_general(a, b, (((1,), (0,)), ((), ())), preferred_element_type=F32)


def dot_nt(a, b):
    return lax.dot_general(a, b, (((1,), (1,)), ((), ())), preferred_element_type=F32)


def cycle_kernel(
    amps_h, ints_h, occ_s, occ_h, virt_h, occ_eh, virt_eh, out,
    occ_r, virt_r, occ_e, virt_e, gain, expand, diff, amps, ints, rows, tsend, w_last, wsend, wstage, tbuf, wring, place, labels, last_rows, gather_last, to_rows, to_owner, row_labels,
    left, w_tail, rpart, rpeer, dsend, dbuf,
    w_send, w_recv, t_send, t_recv, ring_send, ring_recv, sib_send, sib_recv,
    r_send, r_recv, d_send, d_recv, in_sems,
):
    load_ints = pltpu.make_async_copy(ints_h, ints, in_sems.at[0])
    load_amps = pltpu.make_async_copy(amps_h, amps, in_sems.at[1])
    loads = [
        pltpu.make_async_copy(src, dst, in_sems.at[n + 2])
        for n, (src, dst) in enumerate([(occ_h, occ_r), (virt_h, virt_r), (occ_eh, occ_e), (virt_eh, virt_e)])
    ]
    for load in loads:
        load.start()
    load_ints.start()
    load_amps.start()
    o, v = lax.axis_index("occ"), lax.axis_index("virt")
    xh, y = o // 4, lax.rem(o, 4)
    z, s = v // 4, lax.rem(v, 4)
    xl, core = s // 2, lax.rem(s, 2)

    barrier = pltpu.get_barrier_semaphore()
    for sd in range(4):
        def greet(d, _, sd=sd):
            pl.semaphore_signal(barrier, inc=1, device_id=(lax.rem(o + d, 8), z * 4 + lax.rem(s + sd, 4)), device_id_type=MESH)
            return 0
        lax.fori_loop(1 if sd == 0 else 0, 8, greet, 0)
    for zd in (lax.rem(z + 1, 8), lax.rem(z + 7, 8)):
        pl.semaphore_signal(barrier, inc=1, device_id=(o, zd * 4 + s), device_id_type=MESH)

    for load in loads:
        load.wait()
    virt = virt_r[...].reshape(1, 384)
    virtf = virt.astype(F32)
    occf = occ_r[...].reshape(1, 24).astype(F32)
    r0, c0 = iota((384, 384), 0), iota((384, 384), 1)
    vcol = jnp.sum(jnp.where(r0 == c0, virtf, 0.0), axis=1, keepdims=True)
    rank = jnp.sum(jnp.where((vcol == virtf) & (r0 < c0), 1.0, 0.0), axis=0, keepdims=True)
    ranki = rank.astype(I32)

    load_ints.wait()
    b, j = parts_of(iota((288, 1), 0), 24)
    label = pick(virtf, v * 12 + b).astype(I32) ^ pick(occf, j).astype(I32)
    total = jnp.zeros((288, 384), F32)
    for k in range(3):
        w = ints[:, k].astype(F32).reshape(288, 384)
        w = jnp.where((label ^ occ_s[3 * o + k]) == virt, w, 0.0).astype(BF16)
        total += dot_nt(w, one_hot(r0 == ranki + (96 * k + 32 * y)))
    od, r = parts_of(iota((384, 1), 0), 48)
    jl, b = parts_of(r, 12)
    source = jnp.where(r < 36, b * 24 + 3 * od + jl, -1)
    w = dot_nn(one_hot(iota((384, 288), 1) == source), total.astype(BF16))
    w_last[...] = jnp.zeros((8, 16, 128), F32)
    for d in range(8):
        for n in range(3):
            tile = w[d * 48 : d * 48 + 36, n * 128 : n * 128 + 128]
            wsend[d, n * 32 : n * 32 + 32] = tile[0:32].astype(BF16)
            w_last[d, n * 4 : n * 4 + 4] = tile[32:36]
    wsend[:, 96:112] = w_last[...].astype(BF16)

    pl.semaphore_wait(barrier, 33)

    def w_copy(d):
        od = lax.rem(o + d, 8)
        return pltpu.make_async_remote_copy(
            src_ref=wsend.at[od], dst_ref=wstage.at[y * 2 + xl], send_sem=w_send, recv_sem=w_recv,
            device_id=(od, z * 4 + xh * 2 + core), device_id_type=MESH,
        )

    @pl.when(xh == xl)
    def _():
        pltpu.make_async_copy(wsend.at[o], wstage.at[y * 2 + xl], w_recv).start()

    @pl.when(xh != xl)
    def _():
        w_copy(0).start()

    def w_start(d, _):
        w_copy(d).start()
        return 0

    lax.fori_loop(1, 8, w_start, 0)

    def t_copy(d, x):
        xd = lax.rem(xl + x, 2)
        return pltpu.make_async_remote_copy(
            src_ref=tsend.at[xd], dst_ref=tbuf.at[o, xl], send_sem=t_send, recv_sem=t_recv,
            device_id=(lax.rem(o + d, 8), z * 4 + xd * 2 + core), device_id_type=MESH,
        )

    load_amps.wait()
    ia, q = parts_of(iota((216, 1), 0), 6)
    i, a = parts_of(ia, 12)
    label = pick(virtf, v * 12 + a).astype(I32) ^ pick(occf, 3 * o + i).astype(I32)
    for lane in range(3):
        rows[lane] = amps[:, lane * 128 : lane * 128 + 128]
    total = jnp.zeros((216, 384), F32)
    for kk in range(4):
        t = jnp.concatenate([rows[lane, pl.ds(kk, 216, stride=4), :] for lane in range(3)], axis=1)
        t = jnp.where((label ^ pick(occf, 4 * q + kk).astype(I32)) == virt, t, 0.0).astype(BF16)
        total += dot_nt(t, one_hot(r0 == ranki + 96 * kk))
    qd, r = parts_of(iota((288, 1), 0), 48)
    source = jnp.where(r < 36, r * 6 + qd, -1)
    t = dot_nn(one_hot(iota((288, 216), 1) == source), total.astype(BF16))
    last_rows[...] = jnp.zeros((2, 48, 128), F32)
    for q in range(6):
        for lane in range(3):
            tile = t[q * 48 : q * 48 + 36, lane * 128 : lane * 128 + 128]
            n = (q % 3) * 3 + lane
            tsend[q // 3, n * 32 : n * 32 + 32] = tile[0:32].astype(BF16)
            last_rows[q // 3, n * 4 : n * 4 + 4] = tile[32:36]
    tsend[:, 288:336] = last_rows[...].astype(BF16)

    n = iota((288, 1), 0)
    gather_last[...] = one_hot(iota((288, 384), 1) == ((n & 31) >> 2) * 48 + (n >> 5) * 4 + (n & 3))
    x, n = parts_of(n, 144)
    u, r = parts_of(n, 36)
    block = u * 2 + x
    to_rows[...] = one_hot(iota((288, 288), 1) == jnp.where(r < 32, block * 32 + r, 224 + block * 4 + r))
    u, r = parts_of(iota((192, 1), 0), 48)
    i, a = r >> 4, r & 15
    to_owner[...] = one_hot(iota((192, 144), 1) == jnp.where(a < 12, u * 36 + i * 12 + a, -1))

    values = jnp.concatenate([jnp.broadcast_to(rank, (4, 384)), jnp.broadcast_to(virtf, (4, 384))], axis=0).astype(BF16)
    n = iota((1, 1152), 1)
    block = jnp.where(n < 1024, n >> 6, (n - 1024) >> 3)
    zz, c = block >> 1, block & 1
    x = jnp.where(n < 1024, (n & 63) >> 5, (n & 7) >> 2)
    jl, bl = parts_of(jnp.where(n < 1024, n & 31, 32 + (n & 3)), 12)
    b = ((z + zz + 6) & 7) * 48 + x * 24 + c * 12 + bl
    spread = dot_nn(values, one_hot(iota((384, 1152), 0) == b)).astype(I32)
    place[...] = one_hot(iota((384, 1152), 0) == spread[0:1, :] + jl * 128)
    oj = jnp.where(jl == 0, occ_s[3 * o], jnp.where(jl == 1, occ_s[3 * o + 1], occ_s[3 * o + 2]))
    labels[...] = jnp.broadcast_to(spread[4:5, :] ^ oj, (8, 1152))

    x, n = parts_of(iota((288, 1), 0), 144)
    u, r = parts_of(n, 36)
    il, a = parts_of(r, 12)
    label = pick(virtf, z * 48 + x * 24 + core * 12 + a).astype(I32)
    for half in range(2):
        own = label ^ pick(occf, 12 * half + 3 * u + il).astype(I32)
        row_labels[half] = jnp.broadcast_to(own, (288, 128))

    expand[...] = one_hot((iota((256, 384), 0) & 127) == ranki)
    occ_en, virt_en = occ_e[...].reshape(1, 24), virt_e[...].reshape(1, 384)
    for i in range(3):
        a, j = parts_of(iota((288, 1), 0), 24)
        at = pl.ds(i * 288, 288)
        own = jnp.full((288, 1), 3 * o + i)
        label = pick(virtf, v * 12 + a).astype(I32) ^ pick(occf, j).astype(I32) ^ pick(occf, own).astype(I32)
        denom = pick(occ_en, own) + pick(occ_en, j) - pick(virt_en, v * 12 + a) - virt_en
        gain[at, :] = jnp.where(label == virt, 1.0 / denom, 0.0)
        amps[at, :] = jnp.where(label == virt, amps[at, :], 0.0)

    n = iota((96, 1), 0)
    zz, r = parts_of(n, 24)
    gather = one_hot(iota((96, 128), 1) == (zz * 2 + ((r & 7) >> 2)) * 16 + (r >> 3) * 4 + (r & 3))
    pltpu.make_async_copy(wstage, wstage, w_recv).wait()
    tails = dot_nn(gather, wstage[:, 96:112].reshape(128, 128))
    main, tail = [0.0] * 9, [0.0] * 9
    for yy in range(4):
        for n in range(3):
            at = yy * 24 + n * 8
            main[2 * yy + n] += wstage[yy * 2 : yy * 2 + 2, n * 32 : n * 32 + 32].reshape(64, 128).astype(F32)
            tail[2 * yy + n] += tails[at : at + 8]
    for n in range(9):
        wring[2, core, n * 64 : n * 64 + 64] = main[n].astype(BF16)
    wring[2, core, 576:656] = jnp.concatenate(tail + [jnp.zeros((8, 128), F32)], axis=0).astype(BF16)

    def half_block(way, t, c):
        return wring.at[(2 - way * t) % 8, c]

    def piece_of(way, t, g):
        rows_here = pl.ds(448, 208) if isinstance(g, int) else pl.ds(pl.multiple_of(224 * g, 224), 224)
        return wring.at[(2 - way * t) % 8, core, rows_here]

    def ring_copy(way, t, g):
        w = (1 - way) // 2
        return pltpu.make_async_remote_copy(
            src_ref=piece_of(way, t - 1, g), dst_ref=piece_of(way, t, g),
            send_sem=ring_send.at[w * 4 + t - 1], recv_sem=ring_recv.at[w * 12 + 3 * t - 3 + g],
            device_id=(o, lax.rem(z + way + 8, 8) * 4 + s), device_id_type=MESH,
        )

    def ring_arrived(way, t, g):
        ref = piece_of(way, t, g)
        pltpu.make_async_copy(ref, ref, ring_recv.at[(1 - way) // 2 * 12 + 3 * t - 3 + g]).wait()

    def to_sibling(ref, n):
        return pltpu.make_async_remote_copy(
            src_ref=ref, dst_ref=ref, send_sem=sib_send.at[n], recv_sem=sib_recv.at[n],
            device_id=(o, z * 4 + xl * 2 + 1 - core), device_id_type=MESH,
        )

    def sib_copy(way, t, g):
        return to_sibling(piece_of(way, t, g), (1 - way) // 2 * 3 + t if t < 4 else 7)

    def sib_arrived(ref, n):
        pltpu.make_async_copy(ref, ref, sib_recv.at[n]).wait()

    def each(count, body):
        def run(g, _):
            body(g)
            return 0
        lax.fori_loop(0, count - 1, run, 0)
        body(count - 1)

    def begin(g):
        ring_copy(1, 1, g).start()
        ring_copy(-1, 1, g).start()

    each(3, begin)
    to_sibling(wring.at[2, core], 0).start()
    pltpu.make_async_copy(tsend.at[xl], tbuf.at[o, xl], t_recv).start()
    for n in range(15):
        t_copy((n + 1) // 2, (n + 1) % 2).start()
    for t in range(1, 4):
        def pass_on(g, t=t):
            for way in (1, -1):
                ring_arrived(way, t, g)
                if t < 3:
                    ring_copy(way, t + 1, g).start()
                else:
                    @pl.when(core == (1 - way) // 2)
                    def _(way=way):
                        ring_copy(way, 4, g).start()
                sib_copy(way, t, g).start()

        each(3, pass_on)

    pltpu.make_async_copy(tbuf, tbuf, t_recv).wait()

    def near(half, _):
        tiles = tbuf[pl.ds(4 * half, 4)].reshape(8, 336, 128)
        last = dot_nn(gather_last[...], tiles[:, 288:336].reshape(384, 128)).astype(BF16)
        rows36 = jnp.concatenate(
            [
                jnp.concatenate([tiles[:, n * 32 : n * 32 + 32].reshape(256, 128), last[n * 32 : n * 32 + 32]], axis=0)
                for n in range(9)
            ],
            axis=1,
        )
        left[half] = dot_nn(to_rows[...], rows36).astype(BF16)
        return 0

    lax.fori_loop(0, 2, near, 0)

    for way in (1, -1):
        @pl.when(core == (1 - way) // 2)
        def _(way=way):
            def keep(g):
                ring_arrived(way, 4, g)
                sib_copy(way, 4, g).start()

            each(3, keep)
    sib_arrived(wring.at[2, 1 - core], 0)
    for way in (1, -1):
        for t in range(1, 4):
            sib_arrived(half_block(way, t, 1 - core), (1 - way) // 2 * 3 + t)
    sib_arrived(half_block(1, 4, 1 - core), 7)

    def r_copy(c):
        half = lax.rem(xh + c, 2)
        return pltpu.make_async_remote_copy(
            src_ref=rpart.at[1 - xl, half], dst_ref=rpeer.at[half],
            send_sem=r_send.at[c], recv_sem=r_recv.at[c],
            device_id=(o, z * 4 + (1 - xl) * 2 + core), device_id_type=MESH,
        )

    def product(c, _):
        half = lax.rem(xh + c, 2)
        blocks = [wring[:, :, n * 64 : n * 64 + 64].reshape(1024, 128) for n in range(9)]
        right = jnp.concatenate([jnp.concatenate(blocks, axis=1), w_tail[...]], axis=0)
        raw = dot_nt(left[half], right)
        raw = jnp.where(row_labels[half][:, 0:1] == labels[0:1, :], raw, 0.0).astype(BF16)
        both = dot_nt(raw, place[...]).astype(BF16)
        rpart[0, half] = both[0:144]
        rpart[1, half] = both[144:288]
        r_copy(c).start()
        return 0

    last_tiles = wring[:, :, 576:656].astype(F32).reshape(16, 10, 8, 128)
    for n in range(9):
        w_tail[:, n * 128 : n * 128 + 128] = last_tiles[:, n].reshape(128, 128).astype(BF16)
    lax.fori_loop(0, 2, product, 0)

    @pl.when(xh != xl)
    def _():
        w_copy(0).wait_send()

    def sent(d, _):
        w_copy(d).wait_send()
        t_copy(d, 0).wait_send()
        t_copy(d, 1).wait_send()
        return 0

    lax.fori_loop(1, 8, sent, 0)
    t_copy(0, 1).wait_send()
    to_sibling(wring.at[2, core], 0).wait_send()
    for way in (1, -1):
        for t in range(1, 4):
            def left_here(g, way=way, t=t):
                ring_copy(way, t, g).wait_send()
                sib_copy(way, t, g).wait_send()

            each(3, left_here)

        @pl.when(core == (1 - way) // 2)
        def _(way=way):
            def far_left(g):
                ring_copy(way, 4, g).wait_send()
                sib_copy(way, 4, g).wait_send()

            each(3, far_left)

    def d_copy(od, c):
        return pltpu.make_async_remote_copy(
            src_ref=dsend.at[od], dst_ref=dbuf.at[o], send_sem=d_send, recv_sem=d_recv.at[c],
            device_id=(od, v), device_id_type=MESH,
        )

    d_local = pltpu.make_async_copy(dsend.at[o], dbuf.at[o], d_recv.at[0])

    def combine(c, _):
        half = lax.rem(xh + c, 2)
        r_copy(c).wait_recv()
        both = rpart[xl, half].astype(F32) + rpeer[half].astype(F32)
        dsend[pl.ds(4 * half, 4)] = dot_nn(to_owner[...], both.astype(BF16)).astype(BF16).reshape(4, 48, 384)
        for u in range(4):
            od = 4 * half + lax.rem(y + 1 + u, 4)

            @pl.when(od == o)
            def _():
                d_local.start()

            @pl.when(od != o)
            def _(od=od):
                d_copy(od, c).start()
        return 0

    lax.fori_loop(0, 2, combine, 0)

    def change(c, _):
        half = lax.rem(xh + c, 2)
        ref = dbuf.at[pl.ds(4 * half, 4)]
        pltpu.make_async_copy(ref, ref, d_recv.at[c]).wait()
        for u in range(4):
            g = 4 * half + u
            for jl in range(3):
                direct = dbuf[g, :, jl * 128 : jl * 128 + 128].astype(F32)
                for i in range(3):
                    mirror = dsend[g, jl * 16 : jl * 16 + 16, i * 128 : i * 128 + 128]
                    x = direct[i * 16 : i * 16 + 16] - mirror.astype(F32)
                    high = x.astype(BF16)
                    diff[i, 3 * u + jl, :, 0:128] = high
                    diff[i, 3 * u + jl, :, 128:256] = (x - high.astype(F32)).astype(BF16)
        for i in range(3):
            e = dot_nn(diff[i].reshape(192, 256), expand[...])
            for j in range(12):
                for lane in range(3):
                    rows[lane, pl.ds(i * 288 + 12 * half + j, 12, stride=24), :] = e[j * 16 : j * 16 + 12, lane * 128 : lane * 128 + 128]
        return 0

    lax.fori_loop(0, 2, change, 0)
    stores = []
    for i in range(3):
        at = pl.ds(i * 288, 288)
        for lane in range(3):
            to = slice(lane * 128, lane * 128 + 128)
            amps[at, to] = amps[at, to] + rows[lane, at, :] * gain[at, to]
        stores.append(pltpu.make_async_copy(amps.at[at], out.at[at], in_sems.at[i]))
        stores[i].start()

    def d_left(d, _):
        d_copy(lax.rem(o + d, 8), 0).wait_send()
        return 0

    lax.fori_loop(1, 8, d_left, 0)
    for c in range(2):
        r_copy(c).wait_send()
    for store in stores:
        store.wait()


def local(amplitudes, cycle_integrals, occ_energy, virt_energy, occ_irrep, virt_irrep):
    smem = pl.BlockSpec(memory_space=pltpu.SMEM)
    amps = jnp.transpose(amplitudes, (0, 2, 1, 3)).reshape(864, 384)
    ints = jnp.transpose(cycle_integrals, (0, 2, 1, 3))
    dma = pltpu.SemaphoreType.DMA
    hbm = pl.BlockSpec(memory_space=pltpu.HBM)
    out = pl.pallas_call(
        cycle_kernel,
        out_shape=jax.ShapeDtypeStruct((864, 384), F32),
        in_specs=[hbm, hbm, smem, hbm, hbm, hbm, hbm],
        out_specs=hbm,
        scratch_shapes=[
            pltpu.VMEM((24,), I32),
            pltpu.VMEM((384,), I32),
            pltpu.VMEM((24,), F32),
            pltpu.VMEM((384,), F32),
            pltpu.VMEM((864, 384), F32),
            pltpu.VMEM((256, 384), BF16),
            pltpu.VMEM((3, 12, 16, 256), BF16),
            pltpu.VMEM((864, 384), F32),
            pltpu.VMEM((12, 3, 24, 384), BF16),
            pltpu.VMEM((3, 864, 128), F32),
            pltpu.VMEM((2, 336, 128), BF16),
            pltpu.VMEM((8, 16, 128), F32),
            pltpu.VMEM((8, 112, 128), BF16),
            pltpu.VMEM((8, 112, 128), BF16),
            pltpu.VMEM((8, 2, 336, 128), BF16),
            pltpu.VMEM((8, 2, 656, 128), BF16),
            pltpu.VMEM((384, 1152), BF16),
            pltpu.VMEM((8, 1152), I32),
            pltpu.VMEM((2, 48, 128), F32),
            pltpu.VMEM((288, 384), BF16),
            pltpu.VMEM((288, 288), BF16),
            pltpu.VMEM((192, 144), BF16),
            pltpu.VMEM((2, 288, 128), I32),
            pltpu.VMEM((2, 288, 1152), BF16),
            pltpu.VMEM((128, 1152), BF16),
            pltpu.VMEM((2, 2, 144, 384), BF16),
            pltpu.VMEM((2, 144, 384), BF16),
            pltpu.VMEM((8, 48, 384), BF16),
            pltpu.VMEM((8, 48, 384), BF16),
            dma, dma, dma, dma, dma((8,)), dma((24,)), dma((8,)), dma((8,)),
            dma((2,)), dma((2,)), dma, dma((2,)), dma((6,)),
        ],
        compiler_params=pltpu.CompilerParams(
            collective_id=0, has_side_effects=True, vmem_limit_bytes=VMEM_LIMIT
        ),
    )(amps, ints, occ_irrep, occ_irrep, virt_irrep, occ_energy, virt_energy)
    return jnp.transpose(out.reshape(3, 12, 24, 384), (0, 2, 1, 3))


def solution(mesh):
    return jax.shard_map(
        local,
        mesh=mesh,
        in_specs=(P("occ", None, "virt", None), P("virt", None, "occ", None), P(), P(), P(), P()),
        out_specs=P("occ", None, "virt", None),
        check_vma=False,
    )
```
